32 devices in a mesh: dp: 4 (over y, x), expert: 8 (over z, core).
Axes of the slice: x: 2, y: 2, z: 4, core: 2. Of those that a mesh axis runs over, the one named last changes fastest.
Arguments:
- tokens: bfloat16 [4096, 3584], P(('dp', 'expert')), may hold values from -6 to 6
- out_grad: bfloat16 [4096, 3584], P(('dp', 'expert')), may hold values from -1.5 to 1.5
- route: int32 [4096, 8], P(('dp', 'expert')), may hold values from 0 to 255, all different within a row; in each aligned block of 128 rows (0 to 127, 128 to 255, ...) at most 8 rows name the same one
- gate_fixed: int32 [4096, 8], P(('dp', 'expert')), may hold values from 16 to 256
- w_gate: bfloat16 [8, 3584, 256], P('expert'), may hold values from -0.09375 to 0.09375
- w_up: bfloat16 [8, 3584, 256], P('expert'), may hold values from -0.09375 to 0.09375
- w_down: bfloat16 [8, 256, 3584], P('expert'), may hold values from -0.125 to 0.125
- router_bias: float32 [256], replicated, may hold values from -1 to 1
- loads: int32 [32, 256], P(('dp', 'expert')), may hold values from 0 to 189
Outputs:
- token_grad: bfloat16 [4096, 3584], P(('dp', 'expert'))
- gate_grad: float32 [4096, 8], P(('dp', 'expert'))
- grad_gate: bfloat16 [8, 3584, 256], P('expert', 'dp')
- grad_up: bfloat16 [8, 3584, 256], P('expert', 'dp')
- grad_down: bfloat16 [8, 256, 3584], P('expert', None, 'dp')
- new_bias: float32 [256], replicated
The draws below stay inside these ranges and needn't reach their ends.
Inputs may be any that keep to these rules, and one draw needn't show every extreme that they name: `route`: each row names 8 different experts. In the rows of one device no expert is named more than 8 times, a bound that some block reaches.
All inputs are finite; a program needn't handle non-finite values.
Results may differ from the reference program's by a relative error of at most 0.02.
Values may be sent and summed in bfloat16 or wider, within the bound.
No kernel may reach another device: no remote copies, remote signals or barrier semaphores. Data moves between devices by JAX's collectives and lax.ppermute only.
A program may use at most 128 MiB of HBM per device.

```python
import math
import jax
import jax.numpy as jnp
import numpy as np
from jax import lax

D = 3584
FF = 2048
EXPERTS_ALL = 256
TOPK = 8
SPLIT = 8
TOK_DEV = 128
CAP = 8
F_DEV = 256
SOURCES = 32
TOKENS = 4096
N_EXPERT = 8


def draw_loads(key, part):
    base_counts = jax.random.randint(key, (SOURCES, EXPERTS_ALL), 0, 64, dtype=jnp.int32)
    base_counts = base_counts.at[SOURCES - 1, 0].set(63).at[0, 1].set(0)
    rising = (SOURCES - 1 + 2 * jnp.arange(SOURCES, dtype=jnp.int32))[:, None]
    return base_counts * rising // (SOURCES - 1)


def plant(values, key, smallest, high):
    dims = values.shape
    index_at = [jax.random.randint(jax.random.fold_in(key, axis), (), 0, dims[axis]) for axis in range(len(dims))]
    values = values.at[tuple(index_at)].set(smallest)
    longest = dims.index(max(dims))
    index_at[longest] = (index_at[longest] + 1) % dims[longest]
    return values.at[tuple(index_at)].set(high)


def block_levels(stream_key, dims, shards, least, top_value):
    factor_of = 1.0
    for position, blocks in shards:
        draws = jax.random.uniform(jax.random.fold_in(jax.random.fold_in(stream_key, 6), position), (blocks,), jnp.float32, least / len(shards), top_value / len(shards))
        factor_of = factor_of * jnp.repeat(jnp.exp(draws), dims[position] // blocks).reshape((-1,) + (1,) * (len(dims) - 1 - position))
    return factor_of


def shared_out(key, own, number, rows, number_of, top, limit, slope):
    ranking = jax.random.permutation(key, number_of)
    heavy_load, usual = load_shares(number_of, rows * top, limit, slope, True), load_shares(number_of, rows * top, limit, slope, False)
    places = jnp.arange(number_of)

    def named(tallies, offset_by):
        used = int((tallies > 0).sum())
        fixed = max(1, used // 4)
        shifted = fixed + (places - fixed + offset_by * (used - fixed)) % max(1, number_of - fixed)
        return jnp.zeros((number_of,), jnp.int32).at[ranking[jnp.where(places < fixed, places, shifted)]].set(jnp.asarray(tallies, jnp.int32))

    tallies = jnp.where(number % 4 == 0, named(heavy_load, number // 4), named(usual, number - number // 4 - 1))
    mixed = jax.random.permutation(jax.random.fold_in(own, 3), number_of)
    source_of, receiver = mixed[0:number_of // 2 * 2:2], mixed[1:number_of // 2 * 2:2]
    slack = jnp.minimum(tallies[source_of] - 1, limit - tallies[receiver]) // 2
    slack = jnp.where((source_of == ranking[0]) | (receiver == ranking[0]) | (tallies[receiver] == 0), 0, jnp.maximum(slack, 0))
    shifted = jax.random.randint(jax.random.fold_in(own, 4), (number_of // 2,), 0, 1 << 20) % (slack + 1)
    tallies = tallies.at[source_of].add(-shifted).at[receiver].add(shifted)
    items = jnp.searchsorted(jnp.cumsum(tallies), jnp.arange(rows * top), side="right").astype(jnp.int32)
    listing = items.reshape(top, rows).T
    listing = listing[jax.random.permutation(jax.random.fold_in(own, 1), rows)]
    offset_by = jax.random.randint(jax.random.fold_in(own, 2), (rows, 1), 0, top)
    return jnp.take_along_axis(listing, (jnp.arange(top)[None, :] + offset_by) % top, axis=1)


def load_shares(count, total, limit, skew, full):
    weights = [(1 << 20) // math.isqrt(rank ** skew) + 1 for rank in range(1, count + 1)]
    largest = limit if full else min(limit, max(-(-total // count), total * weights[0] // sum(weights)))
    least = 1 if total - largest >= count - 1 else 0
    counts, rest = [largest] + [least] * (count - 1), total - largest - least * (count - 1)
    while rest > 0:
        candidates = [i for i in range(1, count) if counts[i] < largest] or [i for i in range(1, count) if counts[i] < limit]
        whole, remaining = sum([weights[i] for i in candidates]), rest
        for i in candidates:
            extra = min(limit - counts[i], max(1, remaining * weights[i] // whole), rest)
            counts[i] = counts[i] + extra
            rest = rest - extra
    return np.array(counts)


def bell_draw(key, extent, deviation, most, cuts=(), held_as=jnp.bfloat16):
    values = deviation * jax.random.normal(key, extent, jnp.float32)
    if cuts:
        values = values * block_levels(key, extent, cuts, -0.22, 0.18)
    return jnp.clip(values, -most, most).astype(held_as)


def setup_inputs(seed: int = 0) -> dict:
    splits = jax.random.split(jax.random.key(seed), 10)
    tokens = bell_draw(splits[0], (TOKENS, D), 1.0, 6.0, ((0, 32),))
    out_grad = bell_draw(splits[1], (TOKENS, D), 0.25, 1.5, ((0, 32),))
    route_keys = jax.random.split(jax.random.fold_in(splits[2], 1), TOKENS // TOK_DEV)
    route_turns = jax.random.permutation(jax.random.fold_in(splits[2], 3), TOKENS // TOK_DEV)
    route = jax.vmap(lambda own, number: shared_out(jax.random.fold_in(splits[2], 2), own, number, TOK_DEV, EXPERTS_ALL, TOPK, CAP, 1))(route_keys, route_turns).reshape((TOKENS, TOPK))
    gate_fixed = plant(jax.random.randint(splits[3], (TOKENS, TOPK), 16, 257), jax.random.fold_in(splits[3], 1), 16, 256).astype(jnp.int32)
    w_gate = bell_draw(splits[4], (N_EXPERT, D, F_DEV), D ** -0.5, 0.09375, ((0, 8),))
    w_up = bell_draw(splits[5], (N_EXPERT, D, F_DEV), D ** -0.5, 0.09375, ((0, 8),))
    w_down = bell_draw(splits[6], (N_EXPERT, F_DEV, D), FF ** -0.5, 0.125, ((0, 8),))
    router_bias = jnp.clip(jax.random.uniform(splits[7], (EXPERTS_ALL,), jnp.float32, -1.0, 1.0), -1.0, 1.0)
    loads = draw_loads(jax.random.fold_in(splits[9], 71), 0)
    return dict(tokens=tokens, out_grad=out_grad, route=route, gate_fixed=gate_fixed, w_gate=w_gate, w_up=w_up, w_down=w_down, router_bias=router_bias, loads=loads)


bias_step = 0.125


def reference(tokens, out_grad, route, gate_fixed, w_gate, w_up, w_down, router_bias, loads):
    flights = N_EXPERT // SPLIT
    total = TOKENS * TOPK
    most_rows = SOURCES * CAP
    width = tokens.shape[1]
    flat_route = route.reshape(-1)
    flat_gate = gate_fixed.reshape(-1).astype(jnp.float32) / 256.0

    def one_expert(expert_id):
        picked = jnp.nonzero(flat_route == expert_id, size=most_rows, fill_value=total)[0].astype(jnp.int32)
        is_valid = picked < total
        safe_index = jnp.minimum(picked, total - 1)
        token_id = safe_index // TOPK
        rows_in = jnp.where(is_valid[:, None], tokens[token_id], jnp.zeros((), tokens.dtype))
        rows_grad = jnp.where(is_valid[:, None], out_grad[token_id], jnp.zeros((), out_grad.dtype))
        row_gate = jnp.where(is_valid, flat_gate[safe_index], jnp.zeros((), flat_gate.dtype))[:, None]
        first = (expert_id * SPLIT).astype(jnp.int32)
        gate_block = lax.dynamic_slice_in_dim(w_gate, first, SPLIT, 0)
        up_block = lax.dynamic_slice_in_dim(w_up, first, SPLIT, 0)
        down_block = lax.dynamic_slice_in_dim(w_down, first, SPLIT, 0)
        dx_sum = jnp.zeros((most_rows, width), jnp.float32)
        gate_sum = jnp.zeros((most_rows,), jnp.float32)
        grads_g = []
        grads_u = []
        grads_d = []
        for slice_id in range(SPLIT):
            gate_slice = gate_block[slice_id]
            up_slice = up_block[slice_id]
            down_slice = down_block[slice_id]
            pre_gate = jnp.dot(rows_in, gate_slice, preferred_element_type=jnp.float32)
            pre_up = jnp.dot(rows_in, up_slice, preferred_element_type=jnp.float32)
            sigmoid_gate = jax.nn.sigmoid(pre_gate)
            activated = pre_gate * sigmoid_gate
            hidden = activated * pre_up
            back_proj = jnp.dot(rows_grad, down_slice.T, preferred_element_type=jnp.float32)
            part_gate = jnp.sum(back_proj * hidden, axis=1).astype(jnp.bfloat16)
            grad_hidden = row_gate * back_proj
            grad_pregate = (grad_hidden * pre_up * sigmoid_gate * (1.0 + pre_gate * (1.0 - sigmoid_gate))).astype(jnp.bfloat16)
            grad_preup = (grad_hidden * activated).astype(jnp.bfloat16)
            scaled_hidden = (row_gate * hidden).astype(jnp.bfloat16)
            part_dx = (jnp.dot(grad_pregate, gate_slice.T, preferred_element_type=jnp.float32)
                       + jnp.dot(grad_preup, up_slice.T, preferred_element_type=jnp.float32)).astype(jnp.bfloat16)
            dx_sum = dx_sum + part_dx.astype(jnp.float32)
            gate_sum = gate_sum + part_gate.astype(jnp.float32)
            grads_g.append(jnp.dot(rows_in.T, grad_pregate, preferred_element_type=jnp.float32))
            grads_u.append(jnp.dot(rows_in.T, grad_preup, preferred_element_type=jnp.float32))
            grads_d.append(jnp.dot(scaled_hidden.T, rows_grad, preferred_element_type=jnp.float32))
        return dx_sum, gate_sum, picked, jnp.stack(grads_g), jnp.stack(grads_u), jnp.stack(grads_d)

    dx_rows, gate_rows, picked, grad_g, grad_u, grad_d = lax.map(one_expert, jnp.arange(flights, dtype=jnp.int32))
    picked = picked.reshape(-1)
    token_id = jnp.where(picked < total, picked // TOPK, TOKENS).astype(jnp.int32)
    token_grad = jax.ops.segment_sum(dx_rows.reshape(-1, width), token_id, num_segments=TOKENS).astype(jnp.bfloat16)
    gate_grad = jax.ops.segment_sum(gate_rows.reshape(-1), picked, num_segments=total).reshape(TOKENS, TOPK)
    grad_gate = grad_g.reshape(N_EXPERT, width, -1).astype(jnp.bfloat16)
    grad_up = grad_u.reshape(N_EXPERT, width, -1).astype(jnp.bfloat16)
    grad_down = grad_d.reshape(N_EXPERT, -1, width).astype(jnp.bfloat16)
    load = jnp.sum(loads, axis=0)
    overall = jnp.sum(load)
    new_bias = router_bias + bias_step * jnp.sign(overall - EXPERTS_ALL * load).astype(jnp.float32)
    return token_grad, gate_grad, grad_gate, grad_up, grad_down, new_bias
```

```python
import functools

import jax
import jax.numpy as jnp
from jax import lax
from jax.experimental import pallas as pl
from jax.experimental.pallas import tpu as pltpu
from jax.sharding import PartitionSpec as P

EXPERTS_ALL = 256
SPLIT = 8
CAP = 8
BLOCK = 2 * CAP
LANES = 128
bias_step = 0.125

F32 = jnp.float32
BF16 = jnp.bfloat16


def dot(left, right, left_dim, right_dim):
    return lax.dot_general(
        left, right, (((left_dim,), (right_dim,)), ((), ())), preferred_element_type=F32
    )


def call(kernel, outs, args, flops, scratch=()):
    size = sum(a.size * a.dtype.itemsize for a in (*args, *outs))
    return pl.pallas_call(
        kernel,
        out_shape=outs,
        in_specs=[pl.BlockSpec(memory_space=pltpu.VMEM)] * len(args),
        out_specs=[pl.BlockSpec(memory_space=pltpu.VMEM)] * len(outs),
        scratch_shapes=list(scratch),
        compiler_params=pltpu.CompilerParams(vmem_limit_bytes=48 * 1024 * 1024),
        cost_estimate=pl.CostEstimate(flops=flops, bytes_accessed=size, transcendentals=0),
    )(*args)


def select_kernel(flights, tok_ref, grad_ref, route_ref, fixed_ref, loads_ref, pay_ref, sel_ref):
    rows, width = tok_ref.shape
    route, fixed = route_ref[...], fixed_ref[...].astype(F32)
    before = lax.broadcasted_iota(jnp.int32, (rows, rows), 0) < lax.broadcasted_iota(
        jnp.int32, (rows, rows), 1
    )
    before = jnp.where(before, 1.0, 0.0).astype(BF16)
    place = lax.broadcasted_iota(jnp.int32, (CAP, rows), 0).astype(F32)
    picks, gates = [], []
    for flight in range(flights):
        hot = route == flight
        mask = jnp.sum(jnp.where(hot, 1.0, 0.0), axis=0, keepdims=True)
        weight = jnp.sum(jnp.where(hot, fixed, 0.0), axis=0, keepdims=True) * (1.0 / 256.0)
        mask = jnp.broadcast_to(mask, (CAP, rows))
        slot = dot(mask.astype(BF16), before, 1, 0)
        pick = jnp.where(slot == place, mask, 0.0)
        picks.append(pick)
        gates.append(jnp.sum(pick * weight, axis=1, keepdims=True))
    pick = jnp.concatenate(picks, axis=0)
    sel_ref[...] = pick
    rows_in = dot(pick.astype(BF16), tok_ref[...], 1, 0)
    rows_grad = dot(pick.astype(BF16), grad_ref[...], 1, 0)
    loads = loads_ref[...]
    high = loads // LANES
    low = (loads - high * LANES).astype(F32)
    high = high.astype(F32)
    line = lax.broadcasted_iota(jnp.int32, (CAP, LANES), 0)
    lane = lax.broadcasted_iota(jnp.int32, (CAP, LANES), 1)
    counts = jnp.zeros((CAP, LANES), F32)
    for at, part in enumerate((low[:, :LANES], low[:, LANES:], high[:, :LANES], high[:, LANES:])):
        counts = jnp.where(line == at, part, counts)
    for flight in range(flights):
        own = slice(flight * CAP, (flight + 1) * CAP)
        pay_ref[flight, :, :width] = jnp.concatenate([rows_in[own], rows_grad[own]], axis=0).astype(
            BF16
        )
        gate = jnp.where(lane == 0, gates[flight], 0.0)
        pay_ref[flight, :, width:] = jnp.concatenate([gate, counts], axis=0).astype(BF16)


def expert_kernel(blocks, groups, copies, shift, *refs):
    pay_refs, refs = refs[:-(len(groups) + copies + 4)], refs[-(len(groups) + copies + 4):]
    gate_ref, up_ref, down_ref = refs[:3]
    back_refs, share_refs, rows_ref = refs[3 : 3 + len(groups)], refs[3 + len(groups) : -1], refs[-1]
    width = gate_ref.shape[0]
    units = gate_ref.shape[1]
    quarter = width // copies
    half = width // 2
    pays = []
    for ref in pay_refs:
        pay = ref[...].reshape(-1, ref.shape[-1])
        pays.append(pay)
    at = 0
    for pay in pays:
        rows_ref[at : at + pay.shape[0], :] = pay[:, :width]
        at += pay.shape[0]
    extra = jnp.concatenate([pay[:, width:] for pay in pays], axis=0).astype(F32)
    extra = extra.reshape(blocks, BLOCK, LANES)
    row_gate = extra[:, :CAP, :1].reshape(blocks * CAP, 1)
    rows = rows_ref[...]

    def part(values, which):
        return values.reshape(blocks, BLOCK, values.shape[-1])[
            :, which * CAP : (which + 1) * CAP
        ].reshape(blocks * CAP, values.shape[-1])

    pre_gate = part(dot(rows, gate_ref[...], 1, 0), 0)
    pre_up = part(dot(rows, up_ref[...], 1, 0), 0)
    back_proj = part(dot(rows, down_ref[...], 1, 1), 1)
    sigmoid_gate = jax.nn.sigmoid(pre_gate)
    activated = pre_gate * sigmoid_gate
    hidden = activated * pre_up
    part_gate = jnp.sum(back_proj * hidden, axis=1, keepdims=True)
    grad_hidden = row_gate * back_proj
    grad_pregate = grad_hidden * pre_up * sigmoid_gate * (1.0 + pre_gate * (1.0 - sigmoid_gate))
    grad_preup = grad_hidden * activated
    scaled_hidden = row_gate * hidden

    def blocked(values):
        return values.reshape(blocks, CAP, values.shape[-1])

    sums = jnp.sum(extra[:, CAP : CAP + 4], axis=0)
    total = sums[0:2] + sums[2:4] * LANES
    top = jnp.floor(total * (1.0 / LANES**2))
    rest = total - top * LANES**2
    middle = jnp.floor(rest * (1.0 / LANES))
    low = rest - middle * LANES
    line = lax.broadcasted_iota(jnp.int32, (CAP, LANES), 0)
    digits = []
    for lanes in range(2):
        digit = jnp.zeros((CAP, LANES), F32)
        for place, value in enumerate((low, middle, top)):
            digit = jnp.where(line == place, value[lanes : lanes + 1], digit)
        digits.append(digit)
    digits = jnp.concatenate(digits, axis=1)[None]
    if blocks > 1:
        digits = jnp.concatenate([digits, jnp.zeros((blocks - 1, CAP, units), F32)], axis=0)
    left = jnp.concatenate([blocked(grad_pregate), blocked(scaled_hidden)], axis=1)
    right = jnp.concatenate([blocked(grad_preup), digits], axis=1)
    left = left.reshape(blocks * BLOCK, units).astype(BF16)
    right = right.reshape(blocks * BLOCK, units).astype(BF16)
    me = lax.axis_index("dp")
    for step in range(copies):
        to = shift(me, step)
        start = pl.multiple_of(to * quarter, LANES)
        share_refs[step][:, :quarter] = rows_ref[:, pl.ds(start, quarter)]
        share_refs[step][:, quarter : quarter + units] = left
        share_refs[step][:, quarter + units :] = right

    part_dx = dot(grad_pregate.astype(BF16), gate_ref[...], 1, 1) + dot(
        grad_preup.astype(BF16), up_ref[...], 1, 1
    )
    part_dx = blocked(part_dx)
    dx = jnp.concatenate([part_dx[:, :, :half], part_dx[:, :, half:]], axis=1).astype(BF16)
    lane = lax.broadcasted_iota(jnp.int32, (blocks, CAP, LANES), 2)
    tail = jnp.where(lane == 0, blocked(part_gate), 0.0)
    tail = jnp.concatenate([tail, jnp.zeros_like(tail)], axis=1).astype(BF16)
    for ref, members in zip(back_refs, groups):
        for at, block in enumerate(members):
            ref[at, :, :half] = dx[block]
            ref[at, :, half:] = tail[block]


def pair_kernel(mine_ref, other_ref, *out_refs):
    total = mine_ref[...].astype(F32) + other_ref[...].astype(F32)
    for at, ref in enumerate(out_refs):
        ref[...] = total[at].astype(ref.dtype)


def token_kernel(flights, sel_ref, route_ref, *refs):
    part_refs, (token_ref, gate_ref) = refs[:-2], refs[-2:]
    half = token_ref.shape[1] // 2
    total = 0.0
    for ref in part_refs:
        total = total + jnp.sum(ref[...].astype(F32), axis=1)
    total = total.reshape(flights, BLOCK, half + LANES)
    rows = jnp.concatenate([total[:, :CAP, :half], total[:, CAP:, :half]], axis=2)
    rows = rows.reshape(flights * CAP, 2 * half)
    pick = sel_ref[...]
    if flights == 1:
        token_ref[...] = dot(pick.astype(BF16), rows.astype(BF16), 0, 0).astype(BF16)
    else:
        token_ref[...] = lax.dot_general(
            pick,
            rows,
            (((0,), (0,)), ((), ())),
            precision=lax.Precision.HIGHEST,
            preferred_element_type=F32,
        ).astype(BF16)
    gates = jnp.zeros(gate_ref.shape, F32)
    for flight in range(flights):
        value = jnp.sum(
            pick[flight * CAP : (flight + 1) * CAP] * total[flight, :CAP, half : half + 1],
            axis=0,
            keepdims=True,
        )
        gates = jnp.where(route_ref[...] == flight, value, gates)
    gate_ref[...] = gates


def weight_kernel(units, bias_ref, *refs):
    share_refs, (gate_ref, up_ref, down_ref, new_ref) = refs[:-4], refs[-4:]
    quarter = share_refs[0].shape[1] - 2 * units
    rows = jnp.concatenate([ref[:, :quarter] for ref in share_refs], axis=0)
    grads = jnp.concatenate([ref[:, quarter:] for ref in share_refs], axis=0).astype(F32)
    line = lax.broadcasted_iota(jnp.int32, grads.shape, 0)
    is_token = line % BLOCK < CAP
    hidden = jnp.where(is_token, grads, 0.0).astype(BF16)
    scaled = jnp.where(is_token, 0.0, grads)[:, :units].astype(BF16)
    both = dot(rows, hidden, 0, 0)
    gate_ref[0] = both[:, :units].astype(BF16)
    up_ref[0] = both[:, units:].astype(BF16)
    down_ref[0] = dot(scaled, rows, 0, 0).astype(BF16)
    load = jnp.zeros((1, units), F32)
    for ref in share_refs:
        digit = ref[:BLOCK, quarter + units :].astype(F32)[CAP : CAP + 3]
        load = load + digit[0:1] + digit[1:2] * LANES + digit[2:3] * LANES**2
    diff = jnp.sum(load, axis=1, keepdims=True) - EXPERTS_ALL * load
    sign = jnp.where(diff > 0.0, 1.0, jnp.where(diff < 0.0, -1.0, 0.0))
    new_ref[...] = bias_ref[...] + bias_step * sign


def per_device(tokens, out_grad, route, gate_fixed, w_gate, w_up, w_down, router_bias, loads):
    row_count, width = tokens.shape
    top_count = route.shape[1]
    units = w_gate.shape[2]
    sources = lax.axis_size("expert")
    copies = lax.axis_size("dp")
    flights = sources // SPLIT
    half, quarter = width // 2, width // copies
    struct = jax.ShapeDtypeStruct

    payload, pick = call(
        functools.partial(select_kernel, flights),
        [struct((flights, BLOCK, width + LANES), BF16), struct((flights * CAP, row_count), F32)],
        [tokens, out_grad, route.T, gate_fixed.T, loads],
        4 * flights * CAP * row_count * width,
    )

    def swap(values, step):
        return lax.ppermute(values, "expert", [(i, i ^ step) for i in range(sources)])

    if flights == 1:
        near = {step: swap(payload, step) for step in range(2, SPLIT, 2)}
        near[0] = payload
        got = [near[k] if k % 2 == 0 else swap(near[k - 1], 1) for k in range(SPLIT)]
        groups = [list(range(0, SPLIT, 2)), list(range(1, SPLIT, 2))]
    else:
        spread = jnp.broadcast_to(payload[:, None], (flights, SPLIT) + payload.shape[1:])
        spread = spread.reshape((sources,) + payload.shape[1:])
        got = [lax.all_to_all(spread, "expert", split_axis=0, concat_axis=0, tiled=True)]
        groups = [list(range(sources))]

    if copies & (copies - 1) == 0:
        shift = lambda index, step: index ^ step
    else:
        shift = lambda index, step: lax.rem(index + step, copies)
    rows = sources * BLOCK
    outs = call(
        functools.partial(expert_kernel, sources, groups, copies, shift),
        [struct((len(group), BLOCK, half + LANES), BF16) for group in groups]
        + [struct((rows, quarter + 2 * units), BF16)] * copies,
        got + [w_gate[0], w_up[0], w_down[0]],
        8 * rows * width * units,
        [pltpu.VMEM((rows, width), BF16)],
    )
    back, shares = outs[: len(groups)], outs[len(groups) :]

    if flights == 1:
        other = swap(back[1], 1)
        block = (BLOCK, half + LANES)
        sums = call(
            pair_kernel,
            [struct(block, F32)] + [struct(block, BF16)] * 3,
            [back[0], other],
            0,
        )
        parts = [sums[0]] + [swap(sums[at], 2 * at) for at in range(1, 4)]
        parts = [part.reshape((1, 1) + block) for part in parts]
    else:
        parts = lax.all_to_all(back[0], "expert", split_axis=0, concat_axis=0, tiled=True)
        parts = [parts.reshape(flights, SPLIT, BLOCK, half + LANES)]
    sent = [shares[0]]
    for step in range(1, copies):
        pairs = [(i, int(shift(i, step)) if copies & (copies - 1) == 0 else (i + step) % copies) for i in range(copies)]
        sent.append(lax.ppermute(shares[step], "dp", pairs))

    grad_gate, grad_up, grad_down, new_bias = call(
        functools.partial(weight_kernel, units),
        [
            struct((1, quarter, units), BF16),
            struct((1, quarter, units), BF16),
            struct((1, units, quarter), BF16),
            struct((1, EXPERTS_ALL), F32),
        ],
        [router_bias[None]] + sent,
        6 * rows * copies * quarter * units,
    )
    token_grad, gate_grad = call(
        functools.partial(token_kernel, flights),
        [struct((row_count, width), BF16), struct((top_count, row_count), F32)],
        [pick, route.T] + parts,
        2 * flights * CAP * row_count * width,
    )
    return (token_grad, gate_grad.T, grad_gate, grad_up, grad_down, new_bias[0])


def solution(mesh):
    in_specs = (
        P(("dp", "expert"), None),
        P(("dp", "expert"), None),
        P(("dp", "expert"), None),
        P(("dp", "expert"), None),
        P("expert", None, None),
        P("expert", None, None),
        P("expert", None, None),
        P(),
        P(("dp", "expert"), None),
    )
    out_specs = (
        P(("dp", "expert"), None),
        P(("dp", "expert"), None),
        P("expert", "dp", None),
        P("expert", "dp", None),
        P("expert", None, "dp"),
        P(),
    )
    return jax.shard_map(
        per_device, mesh=mesh, in_specs=in_specs, out_specs=out_specs, check_vma=False
    )
```

```python
import functools

import jax
import jax.numpy as jnp
from jax import lax
from jax.experimental import pallas as pl
from jax.experimental.pallas import tpu as pltpu
from jax.sharding import PartitionSpec as P

EXPERTS_ALL = 256
SPLIT = 8
CAP = 8
BLOCK = 2 * CAP
LANES = 128
bias_step = 0.125

F32 = jnp.float32
BF16 = jnp.bfloat16


def dot(left, right, left_dim, right_dim):
    return lax.dot_general(
        left, right, (((left_dim,), (right_dim,)), ((), ())), preferred_element_type=F32
    )


def call(kernel, outs, args, cost, scratch=(), space=pltpu.VMEM, limit=6, after=()):
    if lax.axis_size("expert") > SPLIT:
        limit = 60
    if after:
        inner = kernel

        def kernel(*refs):
            inner(*refs[: len(args)], *refs[len(args) + len(after) :])

    return pl.pallas_call(
        kernel,
        out_shape=outs,
        in_specs=[pl.BlockSpec(memory_space=space)] * len(args)
        + [pl.BlockSpec(memory_space=pl.ANY)] * len(after),
        out_specs=[pl.BlockSpec(memory_space=pltpu.VMEM)] * len(outs),
        scratch_shapes=list(scratch),
        compiler_params=pltpu.CompilerParams(vmem_limit_bytes=limit * 1024 * 1024),
        cost_estimate=pl.CostEstimate(flops=0, bytes_accessed=cost, transcendentals=0),
    )(*args, *after)


def select_kernel(flights, *refs):
    given, (pay_ref, sel_ref), held, sems = refs[:5], refs[5:7], refs[7:12], refs[12]
    copies = [pltpu.make_async_copy(given[at], held[at], sems.at[at]) for at in range(5)]
    for copy in copies:
        copy.start()
    tok_ref, grad_ref, route_ref, fixed_ref, loads_ref = held
    rows, width = tok_ref.shape
    before = lax.broadcasted_iota(jnp.int32, (rows, rows), 0) < lax.broadcasted_iota(
        jnp.int32, (rows, rows), 1
    )
    before = jnp.where(before, 1.0, 0.0).astype(BF16)
    place = lax.broadcasted_iota(jnp.int32, (CAP, rows), 0).astype(F32)
    for copy in copies[2:]:
        copy.wait()
    route, fixed = route_ref[...], fixed_ref[...].astype(F32)
    picks, gates = [], []
    for flight in range(flights):
        hot = route == flight
        mask = jnp.sum(jnp.where(hot, 1.0, 0.0), axis=0, keepdims=True)
        weight = jnp.sum(jnp.where(hot, fixed, 0.0), axis=0, keepdims=True) * (1.0 / 256.0)
        mask = jnp.broadcast_to(mask, (CAP, rows))
        slot = dot(mask.astype(BF16), before, 1, 0)
        pick = jnp.where(slot == place, mask, 0.0)
        picks.append(pick)
        gates.append(jnp.sum(pick * weight, axis=1, keepdims=True))
    pick = jnp.concatenate(picks, axis=0)
    sel_ref[...] = pick
    loads = loads_ref[...]
    high = loads // LANES
    low = (loads - high * LANES).astype(F32)
    high = high.astype(F32)
    line = lax.broadcasted_iota(jnp.int32, (CAP, LANES), 0)
    lane = lax.broadcasted_iota(jnp.int32, (CAP, LANES), 1)
    counts = jnp.zeros((CAP, LANES), F32)
    for at, part in enumerate((low[:, :LANES], low[:, LANES:], high[:, :LANES], high[:, LANES:])):
        counts = jnp.where(line == at, part, counts)
    for flight in range(flights):
        gate = jnp.where(lane == 0, gates[flight], 0.0)
        pay_ref[flight, :, width:] = jnp.concatenate([gate, counts], axis=0).astype(BF16)
    for copy in copies[:2]:
        copy.wait()
    rows_in = dot(pick.astype(BF16), tok_ref[...], 1, 0)
    rows_grad = dot(pick.astype(BF16), grad_ref[...], 1, 0)
    for flight in range(flights):
        own = slice(flight * CAP, (flight + 1) * CAP)
        pay_ref[flight, :, :width] = jnp.concatenate([rows_in[own], rows_grad[own]], axis=0).astype(
            BF16
        )


def quarter_kernel(shift, count, *refs):
    copies = lax.axis_size("dp")
    pay_refs, out_refs, all_refs = refs[:count], refs[count : count + copies], refs[count + copies :]
    quarter = out_refs[0].shape[1] - LANES
    width = quarter * copies
    me = lax.axis_index("dp")
    sums = 0.0
    for ref in pay_refs:
        sums = sums + jnp.sum(ref[:, :, width:].astype(F32), axis=0)
    total = sums[CAP : CAP + 2] + sums[CAP + 2 : CAP + 4] * LANES
    top = jnp.floor(total * (1.0 / LANES**2))
    rest = total - top * LANES**2
    middle = jnp.floor(rest * (1.0 / LANES))
    low = rest - middle * LANES
    line = lax.broadcasted_iota(jnp.int32, (BLOCK, LANES), 0)
    digits = jnp.zeros((BLOCK, LANES), F32)
    for place, value in enumerate((low, middle, top)):
        for lanes in range(2):
            digits = jnp.where(line == 2 * place + lanes, value[lanes : lanes + 1], digits)
    digits = digits.astype(BF16)
    for step, out_ref in enumerate(out_refs):
        start = pl.multiple_of(shift(me, step) * quarter, LANES)
        at = 0
        for ref in pay_refs:
            for block in range(ref.shape[0]):
                out_ref[at : at + BLOCK, :quarter] = ref[block, :, pl.ds(start, quarter)]
                out_ref[at : at + BLOCK, quarter:] = digits if at == 0 else jnp.zeros_like(digits)
                at += BLOCK
    for all_ref in all_refs:
        at = 0
        for ref in pay_refs:
            all_ref[at : at + ref.shape[0]] = ref[...]
            at += ref.shape[0]


def stack_kernel(*refs):
    for at, ref in enumerate(refs[:-1]):
        refs[-1][at] = ref[...]


def fetch_kernel(*refs):
    count = len(refs) // 2
    copies = [
        pltpu.make_async_copy(refs[at], refs[count + at], refs[-1].at[at]) for at in range(count)
    ]
    for copy in copies:
        copy.start()
    for copy in copies:
        copy.wait()


def expert_kernel(blocks, groups, *refs):
    pay_refs, refs = refs[: -(len(groups) + 5)], refs[-(len(groups) + 5) :]
    (gate_ref, up_ref, down_ref), back_refs, (grads_ref, rows_ref) = refs[:3], refs[3:-2], refs[-2:]
    width, units = gate_ref.shape
    half = width // 2
    pays = [ref[...].reshape(-1, ref.shape[-1]) for ref in pay_refs]
    at = 0
    for pay in pays:
        rows_ref[at : at + pay.shape[0], :] = pay[:, :width]
        at += pay.shape[0]
    extra = jnp.concatenate([pay[:, width:] for pay in pays], axis=0).astype(F32)
    extra = extra.reshape(blocks, BLOCK, LANES)
    row_gate = extra[:, :CAP, :1].reshape(blocks * CAP, 1)
    rows = rows_ref[...]

    def part(values, which):
        return values.reshape(blocks, BLOCK, values.shape[-1])[
            :, which * CAP : (which + 1) * CAP
        ].reshape(blocks * CAP, values.shape[-1])

    pre_gate = part(dot(rows, gate_ref[...], 1, 0), 0)
    pre_up = part(dot(rows, up_ref[...], 1, 0), 0)
    back_proj = part(dot(rows, down_ref[...], 1, 1), 1)
    sigmoid_gate = jax.nn.sigmoid(pre_gate)
    activated = pre_gate * sigmoid_gate
    hidden = activated * pre_up
    part_gate = jnp.sum(back_proj * hidden, axis=1, keepdims=True)
    grad_hidden = row_gate * back_proj
    grad_pregate = grad_hidden * pre_up * sigmoid_gate * (1.0 + pre_gate * (1.0 - sigmoid_gate))
    grad_preup = grad_hidden * activated
    scaled_hidden = row_gate * hidden

    grads_ref[...] = jnp.concatenate([grad_pregate, grad_preup, scaled_hidden], axis=1).astype(BF16)
    part_dx = dot(grad_pregate.astype(BF16), gate_ref[...], 1, 1) + dot(
        grad_preup.astype(BF16), up_ref[...], 1, 1
    )
    part_dx = part_dx.reshape(blocks, CAP, width)
    dx = jnp.concatenate([part_dx[:, :, :half], part_dx[:, :, half:]], axis=1).astype(BF16)
    lane = lax.broadcasted_iota(jnp.int32, (blocks, CAP, LANES), 2)
    tail = jnp.where(lane == 0, part_gate.reshape(blocks, CAP, 1), 0.0)
    tail = jnp.concatenate([tail, jnp.zeros_like(tail)], axis=1).astype(BF16)
    at = 0
    for ref in back_refs:
        ref[:, :, :half] = dx[at : at + ref.shape[0]]
        ref[:, :, half:] = tail[at : at + ref.shape[0]]
        at += ref.shape[0]


def pair_kernel(mine_ref, *refs):
    out_refs = refs[-mine_ref.shape[0] :]
    other = jnp.concatenate([ref[...] for ref in refs[: -len(out_refs)]], axis=0)
    total = mine_ref[...].astype(F32) + other.astype(F32)
    for at, ref in enumerate(out_refs):
        ref[...] = total[at].astype(ref.dtype)


def token_kernel(flights, sel_ref, route_ref, *refs):
    part_refs, (token_ref, gate_ref) = refs[:-2], refs[-2:]
    half = token_ref.shape[1] // 2
    total = 0.0
    for ref in part_refs:
        total = total + jnp.sum(ref[...].astype(F32), axis=1)
    total = total.reshape(flights, BLOCK, half + LANES)
    rows = jnp.concatenate([total[:, :CAP, :half], total[:, CAP:, :half]], axis=2)
    rows = rows.reshape(flights * CAP, 2 * half)
    pick = sel_ref[...]
    if flights == 1:
        token_ref[...] = dot(pick.astype(BF16), rows.astype(BF16), 0, 0).astype(BF16)
    else:
        token_ref[...] = lax.dot_general(
            pick,
            rows,
            (((0,), (0,)), ((), ())),
            precision=lax.Precision.HIGHEST,
            preferred_element_type=F32,
        ).astype(BF16)
    gates = jnp.zeros(gate_ref.shape, F32)
    for flight in range(flights):
        value = jnp.sum(
            pick[flight * CAP : (flight + 1) * CAP] * total[flight, :CAP, half : half + 1],
            axis=0,
            keepdims=True,
        )
        gates = jnp.where(route_ref[...] == flight, value, gates)
    gate_ref[...] = gates


def weight_kernel(units, blocks, copies, bias_ref, *refs):
    given, (gate_ref, up_ref, down_ref, new_ref) = refs[:-4], refs[-4:]
    quarter = gate_ref.shape[1]
    grads = [ref[...] for ref in given[:copies]]
    rows = []
    load = jnp.zeros((2, LANES), F32)
    for step in range(copies):
        for ref in given[copies:]:
            ref = ref if len(ref.shape) == 2 else ref.at[step]
            rows.append(ref[:, :quarter])
            digit = ref[:BLOCK, quarter:].astype(F32)
            load = load + digit[0:2] + digit[2:4] * LANES + digit[4:6] * LANES**2
    rows = jnp.concatenate(rows, axis=0)
    hidden, scaled = [], []
    for value in grads:
        value = value.astype(F32)
        value = value.reshape(blocks, CAP, value.shape[1])
        left, right = value[:, :, : 2 * units], value[:, :, 2 * units : 3 * units]
        left = jnp.concatenate([left, jnp.zeros_like(left)], axis=1)
        right = jnp.concatenate([jnp.zeros_like(right), right], axis=1)
        hidden.append(left.reshape(blocks * BLOCK, 2 * units).astype(BF16))
        scaled.append(right.reshape(blocks * BLOCK, units).astype(BF16))
    both = dot(rows, jnp.concatenate(hidden, axis=0), 0, 0)
    gate_ref[0] = both[:, :units].astype(BF16)
    up_ref[0] = both[:, units:].astype(BF16)
    down_ref[0] = dot(jnp.concatenate(scaled, axis=0), rows, 0, 0).astype(BF16)
    load = jnp.concatenate([load[0:1], load[1:2]], axis=1)
    diff = jnp.sum(load, axis=1, keepdims=True) - EXPERTS_ALL * load
    sign = jnp.where(diff > 0.0, 1.0, jnp.where(diff < 0.0, -1.0, 0.0))
    new_ref[...] = bias_ref[...] + bias_step * sign


def per_device(tokens, out_grad, route, gate_fixed, w_gate, w_up, w_down, router_bias, loads):
    row_count, width = tokens.shape
    top_count = route.shape[1]
    units = w_gate.shape[2]
    sources = lax.axis_size("expert")
    copies = lax.axis_size("dp")
    flights = sources // SPLIT
    half, quarter = width // 2, width // copies
    struct = jax.ShapeDtypeStruct

    given = [tokens, out_grad, route.T, gate_fixed.T, loads]
    payload, pick = call(
        functools.partial(select_kernel, flights),
        [struct((flights, BLOCK, width + LANES), BF16), struct((flights * CAP, row_count), F32)],
        given,
        4 * row_count * width,
        [pltpu.VMEM(a.shape, a.dtype) for a in given] + [pltpu.SemaphoreType.DMA((len(given),))],
        pltpu.HBM,
        60,
    )

    weights = [w_gate[0], w_up[0], w_down[0]]
    weights = call(
        fetch_kernel,
        [struct(w.shape, w.dtype) for w in weights],
        weights,
        4 * 10**7,
        [pltpu.SemaphoreType.DMA((len(weights),))],
        pltpu.HBM,
        8,
        after=[pick],
    )

    def swap(values, step):
        return lax.ppermute(values, "expert", [(i, i ^ step) for i in range(sources)])

    if flights == 1:
        near = [payload] + [swap(payload, step) for step in range(2, SPLIT, 2)]
        groups = [SPLIT // 2, SPLIT // 4, SPLIT // 4]
    else:
        spread = jnp.broadcast_to(payload[:, None], (flights, SPLIT) + payload.shape[1:])
        spread = spread.reshape((sources,) + payload.shape[1:])
        near = [lax.all_to_all(spread, "expert", split_axis=0, concat_axis=0, tiled=True)]
        groups = [sources]

    paired = copies & (copies - 1) == 0

    def shift(index, step):
        return index ^ step if paired else (index + step) % copies

    def across(values, step):
        return lax.ppermute(values, "dp", [(i, shift(i, step)) for i in range(copies)])

    rows = sources * BLOCK
    kept = groups[0] * BLOCK
    got = [struct((groups[0],) + payload.shape[1:], BF16)] if flights == 1 else []
    sent = call(
        functools.partial(quarter_kernel, shift, len(near)),
        [struct((kept, quarter + LANES), BF16)] * copies + got,
        near,
        1000,
        after=[weights[2]],
    )
    got = [sent[-1], swap(sent[-1], 1)] if flights == 1 else near
    rows_in = [sent[0]] + [across(sent[step], step) for step in range(1, copies)]

    *back, grads = call(
        functools.partial(expert_kernel, sources, groups),
        [struct((group, BLOCK, half + LANES), BF16) for group in groups]
        + [struct((sources * CAP, 3 * units), BF16)],
        [*got, *weights],
        4 * 10**7,
        [pltpu.VMEM((rows, width), BF16)],
        limit=18,
    )
    grads = [grads] + [across(grads, step) for step in range(1, copies)]

    if flights == 1:
        other = [swap(value, 1) for value in back[1:]]
        block = (BLOCK, half + LANES)
        sums = call(
            pair_kernel,
            [struct(block, F32)] + [struct(block, BF16)] * 3,
            [back[0], *other],
            1000,
            after=rows_in[1:],
        )
        parts = [sums[0]] + [swap(sums[at], 2 * at) for at in range(1, 4)]
        parts = [part.reshape((1, 1) + block) for part in parts]
        rows_in = call(
            stack_kernel,
            [struct((copies,) + rows_in[0].shape, BF16)],
            rows_in,
            1000,
            after=[sums[0]],
        )
        rows_in = [rows_in[0], swap(rows_in[0], 1)]
    else:
        parts = lax.all_to_all(back[0], "expert", split_axis=0, concat_axis=0, tiled=True)
        parts = [parts.reshape(flights, SPLIT, BLOCK, half + LANES)]
        rows_in = [jnp.stack(rows_in)]

    grad_gate, grad_up, grad_down, new_bias = call(
        functools.partial(weight_kernel, units, sources, copies),
        [
            struct((1, quarter, units), BF16),
            struct((1, quarter, units), BF16),
            struct((1, units, quarter), BF16),
            struct((1, EXPERTS_ALL), F32),
        ],
        [router_bias[None], *grads, *rows_in],
        1000,
    )
    token_grad, gate_grad = call(
        functools.partial(token_kernel, flights),
        [struct((row_count, width), BF16), struct((top_count, row_count), F32)],
        [pick, route.T] + parts,
        1000,
    )
    return (token_grad, gate_grad.T, grad_gate, grad_up, grad_down, new_bias[0])


def solution(mesh):
    in_specs = (
        P(("dp", "expert"), None),
        P(("dp", "expert"), None),
        P(("dp", "expert"), None),
        P(("dp", "expert"), None),
        P("expert", None, None),
        P("expert", None, None),
        P("expert", None, None),
        P(),
        P(("dp", "expert"), None),
    )
    out_specs = (
        P(("dp", "expert"), None),
        P(("dp", "expert"), None),
        P("expert", "dp", None),
        P("expert", "dp", None),
        P("expert", None, "dp"),
        P(),
    )
    return jax.shard_map(
        per_device, mesh=mesh, in_specs=in_specs, out_specs=out_specs, check_vma=False
    )
```

```python
import functools

import jax
import jax.numpy as jnp
from jax import lax
from jax.experimental import pallas as pl
from jax.experimental.pallas import tpu as pltpu
from jax.sharding import PartitionSpec as P

EXPERTS_ALL = 256
SPLIT = 8
CAP = 8
BLOCK = 2 * CAP
LANES = 128
bias_step = 0.125

F32 = jnp.float32
BF16 = jnp.bfloat16


def dot(left, right, left_dim, right_dim):
    return lax.dot_general(
        left, right, (((left_dim,), (right_dim,)), ((), ())), preferred_element_type=F32
    )


def call(kernel, outs, args, cost, scratch=(), space=pltpu.VMEM, limit=6, after=()):
    if lax.axis_size("expert") > SPLIT:
        limit = 60
    if after:
        inner = kernel

        def kernel(*refs):
            inner(*refs[: len(args)], *refs[len(args) + len(after) :])

    return pl.pallas_call(
        kernel,
        out_shape=outs,
        in_specs=[pl.BlockSpec(memory_space=space)] * len(args)
        + [pl.BlockSpec(memory_space=pl.ANY)] * len(after),
        out_specs=[pl.BlockSpec(memory_space=pltpu.VMEM)] * len(outs),
        scratch_shapes=list(scratch),
        compiler_params=pltpu.CompilerParams(vmem_limit_bytes=limit * 1024 * 1024),
        cost_estimate=pl.CostEstimate(flops=0, bytes_accessed=cost, transcendentals=0),
    )(*args, *after)


def select_kernel(flights, *refs):
    given, (pay_ref, sel_ref), held, sems = refs[:5], refs[5:7], refs[7:12], refs[12]
    copies = [pltpu.make_async_copy(given[at], held[at], sems.at[at]) for at in range(5)]
    for copy in copies:
        copy.start()
    tok_ref, grad_ref, route_ref, fixed_ref, loads_ref = held
    rows, width = tok_ref.shape
    before = lax.broadcasted_iota(jnp.int32, (rows, rows), 0) < lax.broadcasted_iota(
        jnp.int32, (rows, rows), 1
    )
    before = jnp.where(before, 1.0, 0.0).astype(BF16)
    place = lax.broadcasted_iota(jnp.int32, (CAP, rows), 0).astype(F32)
    for copy in copies[2:]:
        copy.wait()
    route, fixed = route_ref[...], fixed_ref[...].astype(F32)
    picks, gates = [], []
    for flight in range(flights):
        hot = route == flight
        mask = jnp.sum(jnp.where(hot, 1.0, 0.0), axis=0, keepdims=True)
        weight = jnp.sum(jnp.where(hot, fixed, 0.0), axis=0, keepdims=True) * (1.0 / 256.0)
        mask = jnp.broadcast_to(mask, (CAP, rows))
        slot = dot(mask.astype(BF16), before, 1, 0)
        pick = jnp.where(slot == place, mask, 0.0)
        picks.append(pick)
        gates.append(jnp.sum(pick * weight, axis=1, keepdims=True))
    pick = jnp.concatenate(picks, axis=0)
    sel_ref[...] = pick
    loads = loads_ref[...]
    high = loads // LANES
    low = (loads - high * LANES).astype(F32)
    high = high.astype(F32)
    line = lax.broadcasted_iota(jnp.int32, (CAP, LANES), 0)
    lane = lax.broadcasted_iota(jnp.int32, (CAP, LANES), 1)
    counts = jnp.zeros((CAP, LANES), F32)
    for at, part in enumerate((low[:, :LANES], low[:, LANES:], high[:, :LANES], high[:, LANES:])):
        counts = jnp.where(line == at, part, counts)
    for flight in range(flights):
        gate = jnp.where(lane == 0, gates[flight], 0.0)
        pay_ref[flight, :, width:] = jnp.concatenate([gate, counts], axis=0).astype(BF16)
    for copy in copies[:2]:
        copy.wait()
    rows_in = dot(pick.astype(BF16), tok_ref[...], 1, 0)
    rows_grad = dot(pick.astype(BF16), grad_ref[...], 1, 0)
    for flight in range(flights):
        own = slice(flight * CAP, (flight + 1) * CAP)
        pay_ref[flight, :, :width] = jnp.concatenate([rows_in[own], rows_grad[own]], axis=0).astype(
            BF16
        )


def quarter_kernel(shift, count, *refs):
    copies = lax.axis_size("dp")
    pay_refs, out_refs, all_refs = refs[:count], refs[count : count + copies], refs[count + copies :]
    quarter = out_refs[0].shape[1]
    me = lax.axis_index("dp")
    for step, out_ref in enumerate(out_refs):
        start = pl.multiple_of(shift(me, step) * quarter, LANES)
        at = 0
        for ref in pay_refs:
            for block in range(ref.shape[0]):
                out_ref[at : at + BLOCK, :] = ref[block, :, pl.ds(start, quarter)]
                at += BLOCK
    for all_ref in all_refs:
        at = 0
        for ref in pay_refs:
            all_ref[at : at + ref.shape[0]] = ref[...]
            at += ref.shape[0]


def stack_kernel(*refs):
    for at, ref in enumerate(refs[:-1]):
        refs[-1][at] = ref[...]


def turn_kernel(gate_ref, up_ref, down_ref, in_ref, down_turned_ref, in_turned_ref):
    units = gate_ref.shape[1]
    for at, ref in enumerate((gate_ref, up_ref)):
        in_ref[:, at * units : (at + 1) * units] = ref[...]
        in_turned_ref[at * units : (at + 1) * units, :] = ref[...].T
    down_turned_ref[...] = down_ref[...].T


def expert_kernel(blocks, groups, *refs):
    pay_refs, refs = refs[: -(len(groups) + 5)], refs[-(len(groups) + 5) :]
    (in_ref, down_ref, turned_ref), back_refs, (grads_ref, rows_ref) = refs[:3], refs[3:-2], refs[-2:]
    width, units = down_ref.shape
    half = width // 2
    pays = [ref[...].reshape(-1, ref.shape[-1]) for ref in pay_refs]
    at = 0
    for pay in pays:
        rows_ref[at : at + pay.shape[0], :] = pay[:, :width]
        at += pay.shape[0]
    extra = jnp.concatenate([pay[:, width:] for pay in pays], axis=0).astype(F32)
    extra = extra.reshape(blocks, BLOCK, LANES)
    row_gate = extra[:, :CAP, :1].reshape(blocks * CAP, 1)
    rows = rows_ref[...]

    def part(values, which):
        return values.reshape(blocks, BLOCK, values.shape[-1])[
            :, which * CAP : (which + 1) * CAP
        ].reshape(blocks * CAP, values.shape[-1])

    pre = part(dot(rows, in_ref[...], 1, 0), 0)
    pre_gate, pre_up = pre[:, :units], pre[:, units:]
    back_proj = part(dot(rows, down_ref[...], 1, 0), 1)
    sigmoid_gate = jax.nn.sigmoid(pre_gate)
    activated = pre_gate * sigmoid_gate
    hidden = activated * pre_up
    part_gate = jnp.sum(back_proj * hidden, axis=1, keepdims=True)
    grad_hidden = row_gate * back_proj
    grad_pregate = grad_hidden * pre_up * sigmoid_gate * (1.0 + pre_gate * (1.0 - sigmoid_gate))
    grad_preup = grad_hidden * activated
    scaled_hidden = row_gate * hidden

    grad_in = jnp.concatenate([grad_pregate, grad_preup], axis=1).astype(BF16)
    grads_ref[:, : 2 * units] = grad_in
    grads_ref[:, 2 * units : 3 * units] = scaled_hidden.astype(BF16)
    sums = jnp.sum(extra[:, CAP : CAP + 4], axis=0)
    total = sums[0:2] + sums[2:4] * LANES
    top = jnp.floor(total * (1.0 / LANES**2))
    rest = total - top * LANES**2
    middle = jnp.floor(rest * (1.0 / LANES))
    low = rest - middle * LANES
    line = lax.broadcasted_iota(jnp.int32, (blocks * CAP, LANES), 0)
    digits = jnp.zeros((blocks * CAP, LANES), F32)
    for place, value in enumerate((low, middle, top)):
        for lanes in range(2):
            digits = jnp.where(line == 2 * place + lanes, value[lanes : lanes + 1], digits)
    grads_ref[:, 3 * units :] = digits.astype(BF16)
    part_dx = dot(grad_in, turned_ref[...], 1, 0)
    part_dx = part_dx.reshape(blocks, CAP, width)
    dx = jnp.concatenate([part_dx[:, :, :half], part_dx[:, :, half:]], axis=1).astype(BF16)
    lane = lax.broadcasted_iota(jnp.int32, (blocks, CAP, LANES), 2)
    tail = jnp.where(lane == 0, part_gate.reshape(blocks, CAP, 1), 0.0)
    tail = jnp.concatenate([tail, jnp.zeros_like(tail)], axis=1).astype(BF16)
    at = 0
    for ref in back_refs:
        ref[:, :, :half] = dx[at : at + ref.shape[0]]
        ref[:, :, half:] = tail[at : at + ref.shape[0]]
        at += ref.shape[0]


def pair_kernel(mine_ref, *refs):
    out_refs = refs[-mine_ref.shape[0] :]
    other = jnp.concatenate([ref[...] for ref in refs[: -len(out_refs)]], axis=0)
    total = mine_ref[...].astype(F32) + other.astype(F32)
    for at, ref in enumerate(out_refs):
        ref[...] = total[at].astype(ref.dtype)


def token_kernel(flights, sel_ref, route_ref, *refs):
    part_refs, (token_ref, gate_ref) = refs[:-2], refs[-2:]
    half = token_ref.shape[1] // 2
    total = 0.0
    for ref in part_refs:
        total = total + jnp.sum(ref[...].astype(F32), axis=1)
    total = total.reshape(flights, BLOCK, half + LANES)
    rows = jnp.concatenate([total[:, :CAP, :half], total[:, CAP:, :half]], axis=2)
    rows = rows.reshape(flights * CAP, 2 * half)
    pick = sel_ref[...]
    if flights == 1:
        token_ref[...] = dot(pick.astype(BF16), rows.astype(BF16), 0, 0).astype(BF16)
    else:
        token_ref[...] = lax.dot_general(
            pick,
            rows,
            (((0,), (0,)), ((), ())),
            precision=lax.Precision.HIGHEST,
            preferred_element_type=F32,
        ).astype(BF16)
    gates = jnp.zeros(gate_ref.shape, F32)
    for flight in range(flights):
        value = jnp.sum(
            pick[flight * CAP : (flight + 1) * CAP] * total[flight, :CAP, half : half + 1],
            axis=0,
            keepdims=True,
        )
        gates = jnp.where(route_ref[...] == flight, value, gates)
    gate_ref[...] = gates


def weight_kernel(units, blocks, copies, bias_ref, *refs):
    given, (gate_ref, up_ref, down_ref, new_ref) = refs[:-4], refs[-4:]
    quarter = gate_ref.shape[1]
    grads = [ref[...] for ref in given[:copies]]
    rows = []
    load = jnp.zeros((2, LANES), F32)
    for step in range(copies):
        for ref in given[copies:]:
            ref = ref if len(ref.shape) == 2 else ref.at[step]
            rows.append(ref[...])
    rows = jnp.concatenate(rows, axis=0)
    hidden, scaled = [], []
    for value in grads:
        value = value.astype(F32)
        digit = value[:CAP, 3 * units :]
        load = load + digit[0:2] + digit[2:4] * LANES + digit[4:6] * LANES**2
        value = value.reshape(blocks, CAP, value.shape[1])
        left, right = value[:, :, : 2 * units], value[:, :, 2 * units : 3 * units]
        left = jnp.concatenate([left, jnp.zeros_like(left)], axis=1)
        right = jnp.concatenate([jnp.zeros_like(right), right], axis=1)
        hidden.append(left.reshape(blocks * BLOCK, 2 * units).astype(BF16))
        scaled.append(right.reshape(blocks * BLOCK, units).astype(BF16))
    both = dot(rows, jnp.concatenate(hidden, axis=0), 0, 0)
    gate_ref[0] = both[:, :units].astype(BF16)
    up_ref[0] = both[:, units:].astype(BF16)
    down_ref[0] = dot(jnp.concatenate(scaled, axis=0), rows, 0, 0).astype(BF16)
    load = jnp.concatenate([load[0:1], load[1:2]], axis=1)
    diff = jnp.sum(load, axis=1, keepdims=True) - EXPERTS_ALL * load
    sign = jnp.where(diff > 0.0, 1.0, jnp.where(diff < 0.0, -1.0, 0.0))
    new_ref[...] = bias_ref[...] + bias_step * sign


def per_device(tokens, out_grad, route, gate_fixed, w_gate, w_up, w_down, router_bias, loads):
    row_count, width = tokens.shape
    top_count = route.shape[1]
    units = w_gate.shape[2]
    sources = lax.axis_size("expert")
    copies = lax.axis_size("dp")
    flights = sources // SPLIT
    half, quarter = width // 2, width // copies
    struct = jax.ShapeDtypeStruct

    given = [tokens, out_grad, route.T, gate_fixed.T, loads]
    payload, pick = call(
        functools.partial(select_kernel, flights),
        [struct((flights, BLOCK, width + LANES), BF16), struct((flights * CAP, row_count), F32)],
        given,
        4 * row_count * width,
        [pltpu.VMEM(a.shape, a.dtype) for a in given] + [pltpu.SemaphoreType.DMA((len(given),))],
        pltpu.HBM,
        60,
    )

    weights = [w_gate[0], w_up[0], w_down[0]]
    weights = call(
        turn_kernel,
        [
            struct((width, 2 * units), BF16),
            struct((width, units), BF16),
            struct((2 * units, width), BF16),
        ],
        weights,
        4 * 10**7,
        limit=16,
        after=[pick],
    )

    def swap(values, step):
        return lax.ppermute(values, "expert", [(i, i ^ step) for i in range(sources)])

    if flights == 1:
        near = [payload] + [swap(payload, step) for step in range(2, SPLIT, 2)]
        groups = [4, 1, 3]
    else:
        spread = jnp.broadcast_to(payload[:, None], (flights, SPLIT) + payload.shape[1:])
        spread = spread.reshape((sources,) + payload.shape[1:])
        near = [lax.all_to_all(spread, "expert", split_axis=0, concat_axis=0, tiled=True)]
        groups = [sources]

    paired = copies & (copies - 1) == 0

    def shift(index, step):
        return index ^ step if paired else (index + step) % copies

    def across(values, step):
        return lax.ppermute(values, "dp", [(i, shift(i, step)) for i in range(copies)])

    rows = sources * BLOCK
    kept = groups[0] * BLOCK
    got = [struct((groups[0],) + payload.shape[1:], BF16)] if flights == 1 else []
    sent = call(
        functools.partial(quarter_kernel, shift, len(near)),
        [struct((kept, quarter), BF16)] * copies + got,
        near,
        1000,
        after=[weights[2]],
    )
    got = [sent[-1], swap(sent[-1], 1)] if flights == 1 else near
    rows_in = [sent[0]] + [across(sent[step], step) for step in range(1, copies)]

    *back, grads = call(
        functools.partial(expert_kernel, sources, groups),
        [struct((group, BLOCK, half + LANES), BF16) for group in groups]
        + [struct((sources * CAP, 3 * units + LANES), BF16)],
        [*got, *weights],
        4 * 10**7,
        [pltpu.VMEM((rows, width), BF16)],
        limit=18,
    )
    grads = [grads] + [across(grads, step) for step in range(1, copies)]

    if flights == 1:
        other = [swap(value, 1) for value in back[1:]]
        rows_in = call(
            stack_kernel,
            [struct((copies,) + rows_in[0].shape, BF16)],
            rows_in,
            1000,
            after=[other[0]],
        )
        rows_in = [rows_in[0], swap(rows_in[0], 1)]
        block = (BLOCK, half + LANES)
        sums = call(
            pair_kernel,
            [struct(block, F32)] + [struct(block, BF16)] * 3,
            [back[0], *other],
            1000,
            after=[rows_in[1]],
        )
        parts = [sums[0]] + [swap(sums[at], 2 * at) for at in range(1, 4)]
        parts = [part.reshape((1, 1) + block) for part in parts]
    else:
        parts = lax.all_to_all(back[0], "expert", split_axis=0, concat_axis=0, tiled=True)
        parts = [parts.reshape(flights, SPLIT, BLOCK, half + LANES)]
        rows_in = [jnp.stack(rows_in)]

    grad_gate, grad_up, grad_down, new_bias = call(
        functools.partial(weight_kernel, units, sources, copies),
        [
            struct((1, quarter, units), BF16),
            struct((1, quarter, units), BF16),
            struct((1, units, quarter), BF16),
            struct((1, EXPERTS_ALL), F32),
        ],
        [router_bias[None], *grads, *rows_in],
        1000,
    )
    token_grad, gate_grad = call(
        functools.partial(token_kernel, flights),
        [struct((row_count, width), BF16), struct((top_count, row_count), F32)],
        [pick, route.T] + parts,
        1000,
    )
    return (token_grad, gate_grad.T, grad_gate, grad_up, grad_down, new_bias[0])


def solution(mesh):
    in_specs = (
        P(("dp", "expert"), None),
        P(("dp", "expert"), None),
        P(("dp", "expert"), None),
        P(("dp", "expert"), None),
        P("expert", None, None),
        P("expert", None, None),
        P("expert", None, None),
        P(),
        P(("dp", "expert"), None),
    )
    out_specs = (
        P(("dp", "expert"), None),
        P(("dp", "expert"), None),
        P("expert", "dp", None),
        P("expert", "dp", None),
        P("expert", None, "dp"),
        P(),
    )
    return jax.shard_map(
        per_device, mesh=mesh, in_specs=in_specs, out_specs=out_specs, check_vma=False
    )
```

```python
import functools

import jax
import jax.numpy as jnp
from jax import lax
from jax.experimental import pallas as pl
from jax.experimental.pallas import tpu as pltpu
from jax.sharding import PartitionSpec as P

EXPERTS_ALL = 256
SPLIT = 8
CAP = 8
BLOCK = 2 * CAP
LANES = 128
bias_step = 0.125

F32 = jnp.float32
BF16 = jnp.bfloat16


def dot(left, right, left_dim, right_dim):
    return lax.dot_general(
        left, right, (((left_dim,), (right_dim,)), ((), ())), preferred_element_type=F32
    )


def call(kernel, outs, args, cost, scratch=(), space=pltpu.VMEM, limit=6, after=(), order=None):
    if lax.axis_size("expert") > SPLIT:
        limit = 60
    order = order or range(len(args))
    inner = kernel

    def kernel(*refs):
        given = [refs[order.index(at)] for at in range(len(args))]
        inner(*given, *refs[len(args) + len(after) :])

    args = [args[at] for at in order]
    return pl.pallas_call(
        kernel,
        out_shape=outs,
        in_specs=[pl.BlockSpec(memory_space=space)] * len(args)
        + [pl.BlockSpec(memory_space=pl.ANY)] * len(after),
        out_specs=[pl.BlockSpec(memory_space=pltpu.VMEM)] * len(outs),
        scratch_shapes=list(scratch),
        compiler_params=pltpu.CompilerParams(vmem_limit_bytes=limit * 1024 * 1024),
        cost_estimate=pl.CostEstimate(flops=0, bytes_accessed=cost, transcendentals=0),
    )(*args, *after)


def select_kernel(flights, *refs):
    given, (pay_ref, sel_ref), held, sems = refs[:5], refs[5:7], refs[7:12], refs[12]
    copies = [pltpu.make_async_copy(given[at], held[at], sems.at[at]) for at in range(5)]
    for copy in copies:
        copy.start()
    tok_ref, grad_ref, route_ref, fixed_ref, loads_ref = held
    rows, width = tok_ref.shape
    before = lax.broadcasted_iota(jnp.int32, (rows, rows), 0) < lax.broadcasted_iota(
        jnp.int32, (rows, rows), 1
    )
    before = jnp.where(before, 1.0, 0.0).astype(BF16)
    place = lax.broadcasted_iota(jnp.int32, (CAP, rows), 0).astype(F32)
    for copy in copies[2:]:
        copy.wait()
    route, fixed = route_ref[...], fixed_ref[...].astype(F32)
    picks, gates = [], []
    for flight in range(flights):
        hot = route == flight
        mask = jnp.sum(jnp.where(hot, 1.0, 0.0), axis=0, keepdims=True)
        weight = jnp.sum(jnp.where(hot, fixed, 0.0), axis=0, keepdims=True) * (1.0 / 256.0)
        mask = jnp.broadcast_to(mask, (CAP, rows))
        slot = dot(mask.astype(BF16), before, 1, 0)
        pick = jnp.where(slot == place, mask, 0.0)
        picks.append(pick)
        gates.append(jnp.sum(pick * weight, axis=1, keepdims=True))
    pick = jnp.concatenate(picks, axis=0)
    sel_ref[...] = pick
    loads = loads_ref[...]
    high = loads // LANES
    low = (loads - high * LANES).astype(F32)
    high = high.astype(F32)
    line = lax.broadcasted_iota(jnp.int32, (CAP, LANES), 0)
    lane = lax.broadcasted_iota(jnp.int32, (CAP, LANES), 1)
    counts = jnp.zeros((CAP, LANES), F32)
    for at, part in enumerate((low[:, :LANES], low[:, LANES:], high[:, :LANES], high[:, LANES:])):
        counts = jnp.where(line == at, part, counts)
    for flight in range(flights):
        gate = jnp.where(lane == 0, gates[flight], 0.0)
        pay_ref[flight, :, width:] = jnp.concatenate([gate, counts], axis=0).astype(BF16)
    for copy in copies[:2]:
        copy.wait()
    rows_in = dot(pick.astype(BF16), tok_ref[...], 1, 0)
    rows_grad = dot(pick.astype(BF16), grad_ref[...], 1, 0)
    for flight in range(flights):
        own = slice(flight * CAP, (flight + 1) * CAP)
        pay_ref[flight, :, :width] = jnp.concatenate([rows_in[own], rows_grad[own]], axis=0).astype(
            BF16
        )


def quarter_kernel(shift, count, *refs):
    copies = lax.axis_size("dp")
    pay_refs, out_refs, all_refs = refs[:count], refs[count : count + copies], refs[count + copies :]
    quarter = out_refs[0].shape[1]
    me = lax.axis_index("dp")
    for step, out_ref in enumerate(out_refs):
        start = pl.multiple_of(shift(me, step) * quarter, LANES)
        at = 0
        for ref in pay_refs:
            for block in range(ref.shape[0]):
                out_ref[at : at + BLOCK, :] = ref[block, :, pl.ds(start, quarter)]
                at += BLOCK
    for all_ref in all_refs:
        at = 0
        for ref in pay_refs:
            all_ref[at : at + ref.shape[0]] = ref[...]
            at += ref.shape[0]


def stack_kernel(*refs):
    for at, ref in enumerate(refs[:-1]):
        refs[-1][at] = ref[...]


def turn_kernel(gate_ref, up_ref, down_ref, in_ref, down_turned_ref, in_turned_ref):
    units = gate_ref.shape[1]
    for at, ref in enumerate((gate_ref, up_ref)):
        in_ref[:, at * units : (at + 1) * units] = ref[...]
        in_turned_ref[at * units : (at + 1) * units, :] = ref[...].T
    down_turned_ref[...] = down_ref[...].T


def expert_kernel(blocks, groups, *refs):
    pay_refs, refs = refs[: -(len(groups) + 5)], refs[-(len(groups) + 5) :]
    (in_ref, down_ref, turned_ref), back_refs, (grads_ref, rows_ref) = refs[:3], refs[3:-2], refs[-2:]
    width, units = down_ref.shape
    half = width // 2
    pays = [ref[...].reshape(-1, ref.shape[-1]) for ref in pay_refs]
    at = 0
    for pay in pays:
        rows_ref[at : at + pay.shape[0], :] = pay[:, :width]
        at += pay.shape[0]
    extra = jnp.concatenate([pay[:, width:] for pay in pays], axis=0).astype(F32)
    extra = extra.reshape(blocks, BLOCK, LANES)
    row_gate = extra[:, :CAP, :1].reshape(blocks * CAP, 1)
    rows = rows_ref[...]

    def part(values, which):
        return values.reshape(blocks, BLOCK, values.shape[-1])[
            :, which * CAP : (which + 1) * CAP
        ].reshape(blocks * CAP, values.shape[-1])

    pre = part(dot(rows, in_ref[...], 1, 0), 0)
    pre_gate, pre_up = pre[:, :units], pre[:, units:]
    back_proj = part(dot(rows, down_ref[...], 1, 0), 1)
    sigmoid_gate = jax.nn.sigmoid(pre_gate)
    activated = pre_gate * sigmoid_gate
    hidden = activated * pre_up
    part_gate = jnp.sum(back_proj * hidden, axis=1, keepdims=True)
    grad_hidden = row_gate * back_proj
    grad_pregate = grad_hidden * pre_up * sigmoid_gate * (1.0 + pre_gate * (1.0 - sigmoid_gate))
    grad_preup = grad_hidden * activated
    scaled_hidden = row_gate * hidden

    grad_in = jnp.concatenate([grad_pregate, grad_preup], axis=1).astype(BF16)
    grads_ref[:, : 2 * units] = grad_in
    grads_ref[:, 2 * units : 3 * units] = scaled_hidden.astype(BF16)
    sums = jnp.sum(extra[:, CAP : CAP + 4], axis=0)
    total = sums[0:2] + sums[2:4] * LANES
    top = jnp.floor(total * (1.0 / LANES**2))
    rest = total - top * LANES**2
    middle = jnp.floor(rest * (1.0 / LANES))
    low = rest - middle * LANES
    line = lax.broadcasted_iota(jnp.int32, (blocks * CAP, LANES), 0)
    digits = jnp.zeros((blocks * CAP, LANES), F32)
    for place, value in enumerate((low, middle, top)):
        for lanes in range(2):
            digits = jnp.where(line == 2 * place + lanes, value[lanes : lanes + 1], digits)
    grads_ref[:, 3 * units :] = digits.astype(BF16)
    part_dx = dot(grad_in, turned_ref[...], 1, 0)
    part_dx = part_dx.reshape(blocks, CAP, width)
    dx = jnp.concatenate([part_dx[:, :, :half], part_dx[:, :, half:]], axis=1).astype(BF16)
    lane = lax.broadcasted_iota(jnp.int32, (blocks, CAP, LANES), 2)
    tail = jnp.where(lane == 0, part_gate.reshape(blocks, CAP, 1), 0.0)
    tail = jnp.concatenate([tail, jnp.zeros_like(tail)], axis=1).astype(BF16)
    at = 0
    for ref in back_refs:
        ref[:, :, :half] = dx[at : at + ref.shape[0]]
        ref[:, :, half:] = tail[at : at + ref.shape[0]]
        at += ref.shape[0]


def pair_kernel(mine_ref, *refs):
    out_refs = refs[-mine_ref.shape[0] :]
    other = jnp.concatenate([ref[...] for ref in refs[: -len(out_refs)]], axis=0)
    total = mine_ref[...].astype(F32) + other.astype(F32)
    for at, ref in enumerate(out_refs):
        ref[...] = total[at].astype(ref.dtype)


def token_kernel(flights, sel_ref, route_ref, *refs):
    part_refs, (token_ref, gate_ref) = refs[:-2], refs[-2:]
    half = token_ref.shape[1] // 2
    total = 0.0
    for ref in part_refs:
        total = total + jnp.sum(ref[...].astype(F32), axis=1)
    total = total.reshape(flights, BLOCK, half + LANES)
    rows = jnp.concatenate([total[:, :CAP, :half], total[:, CAP:, :half]], axis=2)
    rows = rows.reshape(flights * CAP, 2 * half)
    pick = sel_ref[...]
    if flights == 1:
        token_ref[...] = dot(pick.astype(BF16), rows.astype(BF16), 0, 0).astype(BF16)
    else:
        token_ref[...] = lax.dot_general(
            pick,
            rows,
            (((0,), (0,)), ((), ())),
            precision=lax.Precision.HIGHEST,
            preferred_element_type=F32,
        ).astype(BF16)
    gates = jnp.zeros(gate_ref.shape, F32)
    for flight in range(flights):
        value = jnp.sum(
            pick[flight * CAP : (flight + 1) * CAP] * total[flight, :CAP, half : half + 1],
            axis=0,
            keepdims=True,
        )
        gates = jnp.where(route_ref[...] == flight, value, gates)
    gate_ref[...] = gates


def weight_kernel(units, blocks, copies, bias_ref, *refs):
    given, (gate_ref, up_ref, down_ref, new_ref) = refs[:-4], refs[-4:]
    quarter = gate_ref.shape[1]
    grads = [ref[...] for ref in given[:copies]]
    rows = []
    load = jnp.zeros((2, LANES), F32)
    for step in range(copies):
        for ref in given[copies:]:
            ref = ref if len(ref.shape) == 2 else ref.at[step]
            rows.append(ref[...])
    rows = jnp.concatenate(rows, axis=0)
    hidden, scaled = [], []
    for value in grads:
        value = value.astype(F32)
        digit = value[:CAP, 3 * units :]
        load = load + digit[0:2] + digit[2:4] * LANES + digit[4:6] * LANES**2
        value = value.reshape(blocks, CAP, value.shape[1])
        left, right = value[:, :, : 2 * units], value[:, :, 2 * units : 3 * units]
        left = jnp.concatenate([left, jnp.zeros_like(left)], axis=1)
        right = jnp.concatenate([jnp.zeros_like(right), right], axis=1)
        hidden.append(left.reshape(blocks * BLOCK, 2 * units).astype(BF16))
        scaled.append(right.reshape(blocks * BLOCK, units).astype(BF16))
    both = dot(rows, jnp.concatenate(hidden, axis=0), 0, 0)
    gate_ref[0] = both[:, :units].astype(BF16)
    up_ref[0] = both[:, units:].astype(BF16)
    down_ref[0] = dot(jnp.concatenate(scaled, axis=0), rows, 0, 0).astype(BF16)
    load = jnp.concatenate([load[0:1], load[1:2]], axis=1)
    diff = jnp.sum(load, axis=1, keepdims=True) - EXPERTS_ALL * load
    sign = jnp.where(diff > 0.0, 1.0, jnp.where(diff < 0.0, -1.0, 0.0))
    new_ref[...] = bias_ref[...] + bias_step * sign


def per_device(tokens, out_grad, route, gate_fixed, w_gate, w_up, w_down, router_bias, loads):
    row_count, width = tokens.shape
    top_count = route.shape[1]
    units = w_gate.shape[2]
    sources = lax.axis_size("expert")
    copies = lax.axis_size("dp")
    flights = sources // SPLIT
    half, quarter = width // 2, width // copies
    struct = jax.ShapeDtypeStruct

    given = [tokens, out_grad, route.T, gate_fixed.T, loads]
    payload, pick = call(
        functools.partial(select_kernel, flights),
        [struct((flights, BLOCK, width + LANES), BF16), struct((flights * CAP, row_count), F32)],
        given,
        4 * row_count * width,
        [pltpu.VMEM(a.shape, a.dtype) for a in given] + [pltpu.SemaphoreType.DMA((len(given),))],
        pltpu.HBM,
        60,
    )

    weights = [w_gate[0], w_up[0], w_down[0]]
    weights = call(
        turn_kernel,
        [
            struct((width, 2 * units), BF16),
            struct((width, units), BF16),
            struct((2 * units, width), BF16),
        ],
        weights,
        4 * 10**7,
        limit=16,
        after=[pick],
    )

    def swap(values, step):
        return lax.ppermute(values, "expert", [(i, i ^ step) for i in range(sources)])

    if flights == 1:
        near = [payload] + [swap(payload, step) for step in range(2, SPLIT, 2)]
        groups = [4, 1, 3]
    else:
        spread = jnp.broadcast_to(payload[:, None], (flights, SPLIT) + payload.shape[1:])
        spread = spread.reshape((sources,) + payload.shape[1:])
        near = [lax.all_to_all(spread, "expert", split_axis=0, concat_axis=0, tiled=True)]
        groups = [sources]

    paired = copies & (copies - 1) == 0

    def shift(index, step):
        return index ^ step if paired else (index + step) % copies

    def across(values, step):
        return lax.ppermute(values, "dp", [(i, shift(i, step)) for i in range(copies)])

    rows = sources * BLOCK
    kept = groups[0] * BLOCK
    got = [struct((groups[0],) + payload.shape[1:], BF16)] if flights == 1 else []
    sent = call(
        functools.partial(quarter_kernel, shift, len(near)),
        [struct((kept, quarter), BF16)] * copies + got,
        near,
        1000,
        after=[weights[2]],
        order=[0, 3, 1, 2] if flights == 1 else None,
    )
    got = [sent[-1], swap(sent[-1], 1)] if flights == 1 else near
    rows_in = [sent[0]] + [across(sent[step], step) for step in range(1, copies)]

    *back, grads = call(
        functools.partial(expert_kernel, sources, groups),
        [struct((group, BLOCK, half + LANES), BF16) for group in groups]
        + [struct((sources * CAP, 3 * units + LANES), BF16)],
        [*got, *weights],
        4 * 10**7,
        [pltpu.VMEM((rows, width), BF16)],
        limit=18,
    )
    grads = [grads] + [across(grads, step) for step in range(1, copies)]

    if flights == 1:
        other = [swap(value, 1) for value in back[1:]]
        rows_in = call(
            stack_kernel,
            [struct((copies,) + rows_in[0].shape, BF16)],
            rows_in,
            1000,
            after=[other[0]],
            order=[0, *range(copies - 1, 0, -1)],
        )
        rows_in = [rows_in[0], swap(rows_in[0], 1)]
        block = (BLOCK, half + LANES)
        sums = call(
            pair_kernel,
            [struct(block, F32)] + [struct(block, BF16)] * 3,
            [back[0], *other],
            1000,
            after=[rows_in[1]],
        )
        parts = [sums[0]] + [swap(sums[at], 2 * at) for at in range(1, 4)]
        parts = [part.reshape((1, 1) + block) for part in parts]
    else:
        parts = lax.all_to_all(back[0], "expert", split_axis=0, concat_axis=0, tiled=True)
        parts = [parts.reshape(flights, SPLIT, BLOCK, half + LANES)]
        rows_in = [jnp.stack(rows_in)]

    grad_gate, grad_up, grad_down, new_bias = call(
        functools.partial(weight_kernel, units, sources, copies),
        [
            struct((1, quarter, units), BF16),
            struct((1, quarter, units), BF16),
            struct((1, units, quarter), BF16),
            struct((1, EXPERTS_ALL), F32),
        ],
        [router_bias[None], *grads, *rows_in],
        1000,
    )
    token_grad, gate_grad = call(
        functools.partial(token_kernel, flights),
        [struct((row_count, width), BF16), struct((top_count, row_count), F32)],
        [pick, route.T] + parts,
        1000,
        order=[0, 1, 2, 5, 4, 3] if flights == 1 else None,
    )
    return (token_grad, gate_grad.T, grad_gate, grad_up, grad_down, new_bias[0])


def solution(mesh):
    in_specs = (
        P(("dp", "expert"), None),
        P(("dp", "expert"), None),
        P(("dp", "expert"), None),
        P(("dp", "expert"), None),
        P("expert", None, None),
        P("expert", None, None),
        P("expert", None, None),
        P(),
        P(("dp", "expert"), None),
    )
    out_specs = (
        P(("dp", "expert"), None),
        P(("dp", "expert"), None),
        P("expert", "dp", None),
        P("expert", "dp", None),
        P("expert", None, "dp"),
        P(),
    )
    return jax.shard_map(
        per_device, mesh=mesh, in_specs=in_specs, out_specs=out_specs, check_vma=False
    )
```

```python
import functools

import jax
import jax.numpy as jnp
from jax import lax
from jax.experimental import pallas as pl
from jax.experimental.pallas import tpu as pltpu
from jax.sharding import PartitionSpec as P

EXPERTS_ALL = 256
SPLIT = 8
CAP = 8
BLOCK = 2 * CAP
LANES = 128
bias_step = 0.125

F32 = jnp.float32
BF16 = jnp.bfloat16


def dot(left, right, left_dim, right_dim):
    return lax.dot_general(
        left, right, (((left_dim,), (right_dim,)), ((), ())), preferred_element_type=F32
    )


def call(kernel, outs, args, cost, scratch=(), space=pltpu.VMEM, limit=6, after=(), order=None):
    if lax.axis_size("expert") > SPLIT:
        limit = 60
    order = order or range(len(args))
    inner = kernel

    def kernel(*refs):
        given = [refs[order.index(at)] for at in range(len(args))]
        inner(*given, *refs[len(args) + len(after) :])

    args = [args[at] for at in order]
    return pl.pallas_call(
        kernel,
        out_shape=outs,
        in_specs=[pl.BlockSpec(memory_space=space)] * len(args)
        + [pl.BlockSpec(memory_space=pl.ANY)] * len(after),
        out_specs=[pl.BlockSpec(memory_space=pltpu.VMEM)] * len(outs),
        scratch_shapes=list(scratch),
        compiler_params=pltpu.CompilerParams(vmem_limit_bytes=limit * 1024 * 1024),
        cost_estimate=pl.CostEstimate(flops=0, bytes_accessed=cost, transcendentals=0),
    )(*args, *after)


def select_kernel(flights, *refs):
    given, (pay_ref, sel_ref), held, sems = refs[:5], refs[5:7], refs[7:12], refs[12]
    copies = [pltpu.make_async_copy(given[at], held[at], sems.at[at]) for at in range(5)]
    for copy in copies:
        copy.start()
    tok_ref, grad_ref, route_ref, fixed_ref, loads_ref = held
    rows, width = tok_ref.shape
    before = lax.broadcasted_iota(jnp.int32, (rows, rows), 0) < lax.broadcasted_iota(
        jnp.int32, (rows, rows), 1
    )
    before = jnp.where(before, 1.0, 0.0).astype(BF16)
    place = lax.broadcasted_iota(jnp.int32, (CAP, rows), 0).astype(F32)
    for copy in copies[2:]:
        copy.wait()
    route, fixed = route_ref[...], fixed_ref[...].astype(F32)
    picks, gates = [], []
    for flight in range(flights):
        hot = route == flight
        mask = jnp.sum(jnp.where(hot, 1.0, 0.0), axis=0, keepdims=True)
        weight = jnp.sum(jnp.where(hot, fixed, 0.0), axis=0, keepdims=True) * (1.0 / 256.0)
        mask = jnp.broadcast_to(mask, (CAP, rows))
        slot = dot(mask.astype(BF16), before, 1, 0)
        pick = jnp.where(slot == place, mask, 0.0)
        picks.append(pick)
        gates.append(jnp.sum(pick * weight, axis=1, keepdims=True))
    pick = jnp.concatenate(picks, axis=0)
    sel_ref[...] = pick
    loads = loads_ref[...]
    high = loads // LANES
    low = (loads - high * LANES).astype(F32)
    high = high.astype(F32)
    line = lax.broadcasted_iota(jnp.int32, (CAP, LANES), 0)
    lane = lax.broadcasted_iota(jnp.int32, (CAP, LANES), 1)
    counts = jnp.zeros((CAP, LANES), F32)
    for at, part in enumerate((low[:, :LANES], low[:, LANES:], high[:, :LANES], high[:, LANES:])):
        counts = jnp.where(line == at, part, counts)
    for flight in range(flights):
        gate = jnp.where(lane == 0, gates[flight], 0.0)
        pay_ref[flight, :, width:] = jnp.concatenate([gate, counts], axis=0).astype(BF16)
    for copy in copies[:2]:
        copy.wait()
    rows_in = dot(pick.astype(BF16), tok_ref[...], 1, 0)
    rows_grad = dot(pick.astype(BF16), grad_ref[...], 1, 0)
    for flight in range(flights):
        own = slice(flight * CAP, (flight + 1) * CAP)
        pay_ref[flight, :, :width] = jnp.concatenate([rows_in[own], rows_grad[own]], axis=0).astype(
            BF16
        )


def stack_kernel(kept, *refs):
    at = 0
    for ref in refs[:-1]:
        value = ref[...] if kept is None else ref[:kept][None]
        refs[-1][at : at + value.shape[0]] = value
        at += value.shape[0]


def turn_kernel(gate_ref, up_ref, down_ref, in_ref, down_turned_ref, in_turned_ref):
    units = gate_ref.shape[1]
    for at, ref in enumerate((gate_ref, up_ref)):
        in_ref[:, at * units : (at + 1) * units] = ref[...]
        in_turned_ref[at * units : (at + 1) * units, :] = ref[...].T
    down_turned_ref[...] = down_ref[...].T


def expert_kernel(blocks, groups, copies, shift, *refs):
    count = 3 + len(groups) + copies + 2
    pay_refs, refs = refs[:-count], refs[-count:]
    (in_ref, down_ref, turned_ref), refs = refs[:3], refs[3:]
    back_refs, share_refs = refs[: len(groups)], refs[len(groups) : -3]
    own_rows_ref, grads_ref, rows_ref = refs[-3:]
    width, units = down_ref.shape
    half = width // 2
    quarter = width // copies
    pays = [ref[...].reshape(-1, ref.shape[-1]) for ref in pay_refs]
    at = 0
    for pay in pays:
        rows_ref[at : at + pay.shape[0], :] = pay[:, :width]
        at += pay.shape[0]
    extra = jnp.concatenate([pay[:, width:] for pay in pays], axis=0).astype(F32)
    extra = extra.reshape(blocks, BLOCK, LANES)
    row_gate = extra[:, :CAP, :1].reshape(blocks * CAP, 1)
    rows = rows_ref[...]

    def part(values, which):
        return values.reshape(blocks, BLOCK, values.shape[-1])[
            :, which * CAP : (which + 1) * CAP
        ].reshape(blocks * CAP, values.shape[-1])

    pre = part(dot(rows, in_ref[...], 1, 0), 0)
    pre_gate, pre_up = pre[:, :units], pre[:, units:]
    back_proj = part(dot(rows, down_ref[...], 1, 0), 1)
    sigmoid_gate = jax.nn.sigmoid(pre_gate)
    activated = pre_gate * sigmoid_gate
    hidden = activated * pre_up
    part_gate = jnp.sum(back_proj * hidden, axis=1, keepdims=True)
    grad_hidden = row_gate * back_proj
    grad_pregate = grad_hidden * pre_up * sigmoid_gate * (1.0 + pre_gate * (1.0 - sigmoid_gate))
    grad_preup = grad_hidden * activated
    scaled_hidden = row_gate * hidden

    grad_in = jnp.concatenate([grad_pregate, grad_preup], axis=1).astype(BF16)
    grads_ref[:, : 2 * units] = grad_in
    grads_ref[:, 2 * units : 3 * units] = scaled_hidden.astype(BF16)
    sums = jnp.sum(extra[:, CAP : CAP + 4], axis=0)
    total = sums[0:2] + sums[2:4] * LANES
    top = jnp.floor(total * (1.0 / LANES**2))
    rest = total - top * LANES**2
    middle = jnp.floor(rest * (1.0 / LANES))
    low = rest - middle * LANES
    line = lax.broadcasted_iota(jnp.int32, (blocks * CAP, LANES), 0)
    digits = jnp.zeros((blocks * CAP, LANES), F32)
    for place, value in enumerate((low, middle, top)):
        for lanes in range(2):
            digits = jnp.where(line == 2 * place + lanes, value[lanes : lanes + 1], digits)
    grads_ref[:, 3 * units :] = digits.astype(BF16)
    me = lax.axis_index("dp")
    own_rows_ref[...] = rows_ref[:, pl.ds(pl.multiple_of(me * quarter, LANES), quarter)]
    for step, ref in enumerate(share_refs, 1):
        start = pl.multiple_of(shift(me, step) * quarter, LANES)
        sent = ref.shape[0] - blocks * CAP
        ref[:sent, :quarter] = rows_ref[:sent, pl.ds(start, quarter)]
        ref[sent:, : grads_ref.shape[1]] = grads_ref[...]
    part_dx = dot(grad_in, turned_ref[...], 1, 0)
    part_dx = part_dx.reshape(blocks, CAP, width)
    dx = jnp.concatenate([part_dx[:, :, :half], part_dx[:, :, half:]], axis=1).astype(BF16)
    lane = lax.broadcasted_iota(jnp.int32, (blocks, CAP, LANES), 2)
    tail = jnp.where(lane == 0, part_gate.reshape(blocks, CAP, 1), 0.0)
    tail = jnp.concatenate([tail, jnp.zeros_like(tail)], axis=1).astype(BF16)
    at = 0
    for ref in back_refs:
        ref[:, :, :half] = dx[at : at + ref.shape[0]]
        ref[:, :, half:] = tail[at : at + ref.shape[0]]
        at += ref.shape[0]


def pair_kernel(mine_ref, *refs):
    out_refs = refs[-mine_ref.shape[0] :]
    other = jnp.concatenate([ref[...] for ref in refs[: -len(out_refs)]], axis=0)
    total = mine_ref[...].astype(F32) + other.astype(F32)
    for at, ref in enumerate(out_refs):
        ref[...] = total[at].astype(ref.dtype)


def token_kernel(flights, sel_ref, route_ref, *refs):
    part_refs, (token_ref, gate_ref) = refs[:-2], refs[-2:]
    half = token_ref.shape[1] // 2
    total = 0.0
    for ref in part_refs:
        total = total + jnp.sum(ref[...].astype(F32), axis=1)
    total = total.reshape(flights, BLOCK, half + LANES)
    rows = jnp.concatenate([total[:, :CAP, :half], total[:, CAP:, :half]], axis=2)
    rows = rows.reshape(flights * CAP, 2 * half)
    pick = sel_ref[...]
    if flights == 1:
        token_ref[...] = dot(pick.astype(BF16), rows.astype(BF16), 0, 0).astype(BF16)
    else:
        token_ref[...] = lax.dot_general(
            pick,
            rows,
            (((0,), (0,)), ((), ())),
            precision=lax.Precision.HIGHEST,
            preferred_element_type=F32,
        ).astype(BF16)
    gates = jnp.zeros(gate_ref.shape, F32)
    for flight in range(flights):
        value = jnp.sum(
            pick[flight * CAP : (flight + 1) * CAP] * total[flight, :CAP, half : half + 1],
            axis=0,
            keepdims=True,
        )
        gates = jnp.where(route_ref[...] == flight, value, gates)
    gate_ref[...] = gates


def weight_kernel(units, blocks, copies, bias_ref, *refs):
    given, (gate_ref, up_ref, down_ref, new_ref) = refs[:-4], refs[-4:]
    quarter = gate_ref.shape[1]
    rows, grads = [given[0][...]], [given[1][...]]
    for step, ref in enumerate(given[2 : 1 + copies]):
        sent = ref.shape[0] - blocks * CAP
        rows.append(ref[:sent, :quarter])
        grads.append(ref[sent:, :])
        rows += [other[step, :, :quarter] for other in given[1 + copies :]]
    load = jnp.zeros((2, LANES), F32)
    rows = jnp.concatenate(rows, axis=0)
    hidden, scaled = [], []
    for value in grads:
        value = value.astype(F32)
        digit = value[:CAP, 3 * units :]
        load = load + digit[0:2] + digit[2:4] * LANES + digit[4:6] * LANES**2
        value = value.reshape(blocks, CAP, value.shape[1])
        left, right = value[:, :, : 2 * units], value[:, :, 2 * units : 3 * units]
        left = jnp.concatenate([left, jnp.zeros_like(left)], axis=1)
        right = jnp.concatenate([jnp.zeros_like(right), right], axis=1)
        hidden.append(left.reshape(blocks * BLOCK, 2 * units).astype(BF16))
        scaled.append(right.reshape(blocks * BLOCK, units).astype(BF16))
    both = dot(rows, jnp.concatenate(hidden, axis=0), 0, 0)
    gate_ref[0] = both[:, :units].astype(BF16)
    up_ref[0] = both[:, units:].astype(BF16)
    down_ref[0] = dot(jnp.concatenate(scaled, axis=0), rows, 0, 0).astype(BF16)
    load = jnp.concatenate([load[0:1], load[1:2]], axis=1)
    diff = jnp.sum(load, axis=1, keepdims=True) - EXPERTS_ALL * load
    sign = jnp.where(diff > 0.0, 1.0, jnp.where(diff < 0.0, -1.0, 0.0))
    new_ref[...] = bias_ref[...] + bias_step * sign


def per_device(tokens, out_grad, route, gate_fixed, w_gate, w_up, w_down, router_bias, loads):
    row_count, width = tokens.shape
    top_count = route.shape[1]
    units = w_gate.shape[2]
    sources = lax.axis_size("expert")
    copies = lax.axis_size("dp")
    flights = sources // SPLIT
    half, quarter = width // 2, width // copies
    struct = jax.ShapeDtypeStruct

    given = [tokens, out_grad, route.T, gate_fixed.T, loads]
    payload, pick = call(
        functools.partial(select_kernel, flights),
        [struct((flights, BLOCK, width + LANES), BF16), struct((flights * CAP, row_count), F32)],
        given,
        4 * row_count * width,
        [pltpu.VMEM(a.shape, a.dtype) for a in given] + [pltpu.SemaphoreType.DMA((len(given),))],
        pltpu.HBM,
        60,
    )

    weights = [w_gate[0], w_up[0], w_down[0]]
    weights = call(
        turn_kernel,
        [
            struct((width, 2 * units), BF16),
            struct((width, units), BF16),
            struct((2 * units, width), BF16),
        ],
        weights,
        4 * 10**7,
        limit=16,
        after=[pick],
    )

    def swap(values, step):
        return lax.ppermute(values, "expert", [(i, i ^ step) for i in range(sources)])

    if flights == 1:
        near = [payload] + [swap(payload, step) for step in range(2, SPLIT, 2)]
        groups = [SPLIT // 2, SPLIT // 2]
    else:
        spread = jnp.broadcast_to(payload[:, None], (flights, SPLIT) + payload.shape[1:])
        spread = spread.reshape((sources,) + payload.shape[1:])
        near = [lax.all_to_all(spread, "expert", split_axis=0, concat_axis=0, tiled=True)]
        groups = [sources]

    paired = copies & (copies - 1) == 0

    def shift(index, step):
        return index ^ step if paired else (index + step) % copies

    def across(values, step):
        return lax.ppermute(values, "dp", [(i, shift(i, step)) for i in range(copies)])

    rows = sources * BLOCK
    kept = groups[0] * BLOCK
    got = near
    if flights == 1:
        (near,) = call(
            functools.partial(stack_kernel, None),
            [struct((groups[0],) + payload.shape[1:], BF16)],
            near,
            1000,
            after=[weights[2]],
            order=[0, 3, 1, 2],
        )
        got = [near, swap(near, 1)]

    wide = max(quarter, 3 * units + LANES)
    outs = call(
        functools.partial(expert_kernel, sources, groups, copies, shift),
        [struct((group, BLOCK, half + LANES), BF16) for group in groups]
        + [struct((kept + sources * CAP, wide), BF16)] * (copies - 1)
        + [struct((rows, quarter), BF16), struct((sources * CAP, 3 * units + LANES), BF16)],
        [*got, *weights],
        4 * 10**7,
        [pltpu.VMEM((rows, width), BF16)],
        limit=18,
    )
    back, shares, own = outs[: len(groups)], outs[len(groups) : -2], outs[-2:]
    shares = [across(value, step) for step, value in enumerate(shares, 1)]

    if flights == 1:
        other = [swap(value, 1) for value in back[1:]]
        block = (BLOCK, half + LANES)
        sums = call(
            pair_kernel,
            [struct(block, F32)] + [struct(block, BF16)] * 3,
            [back[0], *other],
            1000,
        )
        parts = [sums[0]] + [swap(sums[at], 2 * at) for at in range(1, 4)]
        parts = [part.reshape((1, 1) + block) for part in parts]
        (rows_in,) = call(
            functools.partial(stack_kernel, kept),
            [struct((copies - 1, kept, wide), BF16)],
            shares,
            1000,
            after=parts[1:],
            order=[*range(copies - 2, -1, -1)],
        )
        shares = [*shares, swap(rows_in, 1)]
    else:
        parts = lax.all_to_all(back[0], "expert", split_axis=0, concat_axis=0, tiled=True)
        parts = [parts.reshape(flights, SPLIT, BLOCK, half + LANES)]
    grad_gate, grad_up, grad_down, new_bias = call(
        functools.partial(weight_kernel, units, sources, copies),
        [
            struct((1, quarter, units), BF16),
            struct((1, quarter, units), BF16),
            struct((1, units, quarter), BF16),
            struct((1, EXPERTS_ALL), F32),
        ],
        [router_bias[None], *own, *shares],
        1000,
    )
    token_grad, gate_grad = call(
        functools.partial(token_kernel, flights),
        [struct((row_count, width), BF16), struct((top_count, row_count), F32)],
        [pick, route.T] + parts,
        1000,
        order=[0, 1, 2, 5, 4, 3] if flights == 1 else None,
    )
    return (token_grad, gate_grad.T, grad_gate, grad_up, grad_down, new_bias[0])


def solution(mesh):
    in_specs = (
        P(("dp", "expert"), None),
        P(("dp", "expert"), None),
        P(("dp", "expert"), None),
        P(("dp", "expert"), None),
        P("expert", None, None),
        P("expert", None, None),
        P("expert", None, None),
        P(),
        P(("dp", "expert"), None),
    )
    out_specs = (
        P(("dp", "expert"), None),
        P(("dp", "expert"), None),
        P("expert", "dp", None),
        P("expert", "dp", None),
        P("expert", None, "dp"),
        P(),
    )
    return jax.shard_map(
        per_device, mesh=mesh, in_specs=in_specs, out_specs=out_specs, check_vma=False
    )
```

```python
import functools

import jax
import jax.numpy as jnp
from jax import lax
from jax.experimental import pallas as pl
from jax.experimental.pallas import tpu as pltpu
from jax.sharding import PartitionSpec as P

EXPERTS_ALL = 256
SPLIT = 8
CAP = 8
BLOCK = 2 * CAP
LANES = 128
bias_step = 0.125

F32 = jnp.float32
BF16 = jnp.bfloat16


def dot(left, right, left_dim, right_dim):
    return lax.dot_general(
        left, right, (((left_dim,), (right_dim,)), ((), ())), preferred_element_type=F32
    )


def call(kernel, outs, args, cost, scratch=(), space=pltpu.VMEM, limit=6, after=(), order=None):
    if lax.axis_size("expert") > SPLIT:
        limit = 60
    order = order or range(len(args))
    inner = kernel

    def kernel(*refs):
        given = [refs[order.index(at)] for at in range(len(args))]
        inner(*given, *refs[len(args) + len(after) :])

    args = [args[at] for at in order]
    return pl.pallas_call(
        kernel,
        out_shape=outs,
        in_specs=[pl.BlockSpec(memory_space=space)] * len(args)
        + [pl.BlockSpec(memory_space=pl.ANY)] * len(after),
        out_specs=[pl.BlockSpec(memory_space=pltpu.VMEM)] * len(outs),
        scratch_shapes=list(scratch),
        compiler_params=pltpu.CompilerParams(vmem_limit_bytes=limit * 1024 * 1024),
        cost_estimate=pl.CostEstimate(flops=0, bytes_accessed=cost, transcendentals=0),
    )(*args, *after)


def select_kernel(flights, *refs):
    given, (pay_ref, sel_ref), held, sems = refs[:5], refs[5:7], refs[7:12], refs[12]
    copies = [pltpu.make_async_copy(given[at], held[at], sems.at[at]) for at in range(5)]
    for copy in copies:
        copy.start()
    tok_ref, grad_ref, route_ref, fixed_ref, loads_ref = held
    rows, width = tok_ref.shape
    before = lax.broadcasted_iota(jnp.int32, (rows, rows), 0) < lax.broadcasted_iota(
        jnp.int32, (rows, rows), 1
    )
    before = jnp.where(before, 1.0, 0.0).astype(BF16)
    place = lax.broadcasted_iota(jnp.int32, (CAP, rows), 0).astype(F32)
    for copy in copies[2:]:
        copy.wait()
    route, fixed = route_ref[...], fixed_ref[...].astype(F32)
    picks, gates = [], []
    for flight in range(flights):
        hot = route == flight
        mask = jnp.sum(jnp.where(hot, 1.0, 0.0), axis=0, keepdims=True)
        weight = jnp.sum(jnp.where(hot, fixed, 0.0), axis=0, keepdims=True) * (1.0 / 256.0)
        mask = jnp.broadcast_to(mask, (CAP, rows))
        slot = dot(mask.astype(BF16), before, 1, 0)
        pick = jnp.where(slot == place, mask, 0.0)
        picks.append(pick)
        gates.append(jnp.sum(pick * weight, axis=1, keepdims=True))
    pick = jnp.concatenate(picks, axis=0)
    sel_ref[...] = pick
    loads = loads_ref[...]
    high = loads // LANES
    low = (loads - high * LANES).astype(F32)
    high = high.astype(F32)
    line = lax.broadcasted_iota(jnp.int32, (CAP, LANES), 0)
    lane = lax.broadcasted_iota(jnp.int32, (CAP, LANES), 1)
    counts = jnp.zeros((CAP, LANES), F32)
    for at, part in enumerate((low[:, :LANES], low[:, LANES:], high[:, :LANES], high[:, LANES:])):
        counts = jnp.where(line == at, part, counts)
    for flight in range(flights):
        gate = jnp.where(lane == 0, gates[flight], 0.0)
        pay_ref[flight, :, width:] = jnp.concatenate([gate, counts], axis=0).astype(BF16)
    for copy in copies[:2]:
        copy.wait()
    rows_in = dot(pick.astype(BF16), tok_ref[...], 1, 0)
    rows_grad = dot(pick.astype(BF16), grad_ref[...], 1, 0)
    for flight in range(flights):
        own = slice(flight * CAP, (flight + 1) * CAP)
        pay_ref[flight, :, :width] = jnp.concatenate([rows_in[own], rows_grad[own]], axis=0).astype(
            BF16
        )


def stack_kernel(kept, *refs):
    at = 0
    for ref in refs[:-1]:
        value = ref[...] if kept is None else ref[:kept][None]
        refs[-1][at : at + value.shape[0]] = value
        at += value.shape[0]


def turn_kernel(gate_ref, up_ref, down_ref, in_ref, down_turned_ref, in_turned_ref):
    units = gate_ref.shape[1]
    for at, ref in enumerate((gate_ref, up_ref)):
        in_ref[:, at * units : (at + 1) * units] = ref[...]
        in_turned_ref[at * units : (at + 1) * units, :] = ref[...].T
    down_turned_ref[...] = down_ref[...].T


def expert_kernel(blocks, groups, copies, shift, *refs):
    count = 3 + len(groups) + copies + 2
    pay_refs, refs = refs[:-count], refs[-count:]
    (in_ref, down_ref, turned_ref), refs = refs[:3], refs[3:]
    back_refs, share_refs = refs[: len(groups)], refs[len(groups) : -3]
    own_rows_ref, grads_ref, rows_ref = refs[-3:]
    width, units = down_ref.shape
    half = width // 2
    quarter = width // copies
    pays = [ref[...].reshape(-1, ref.shape[-1]) for ref in pay_refs]
    at = 0
    for pay in pays:
        rows_ref[at : at + pay.shape[0], :] = pay[:, :width]
        at += pay.shape[0]
    extra = jnp.concatenate([pay[:, width:] for pay in pays], axis=0).astype(F32)
    extra = extra.reshape(blocks, BLOCK, LANES)
    row_gate = extra[:, :CAP, :1].reshape(blocks * CAP, 1)
    rows = rows_ref[...]

    def part(values, which):
        return values.reshape(blocks, BLOCK, values.shape[-1])[
            :, which * CAP : (which + 1) * CAP
        ].reshape(blocks * CAP, values.shape[-1])

    pre = part(dot(rows, in_ref[...], 1, 0), 0)
    pre_gate, pre_up = pre[:, :units], pre[:, units:]
    back_proj = part(dot(rows, down_ref[...], 1, 0), 1)
    sigmoid_gate = jax.nn.sigmoid(pre_gate)
    activated = pre_gate * sigmoid_gate
    hidden = activated * pre_up
    part_gate = jnp.sum(back_proj * hidden, axis=1, keepdims=True)
    grad_hidden = row_gate * back_proj
    grad_pregate = grad_hidden * pre_up * sigmoid_gate * (1.0 + pre_gate * (1.0 - sigmoid_gate))
    grad_preup = grad_hidden * activated
    scaled_hidden = row_gate * hidden

    grad_in = jnp.concatenate([grad_pregate, grad_preup], axis=1).astype(BF16)
    grads_ref[:, : 2 * units] = grad_in
    grads_ref[:, 2 * units : 3 * units] = scaled_hidden.astype(BF16)
    sums = jnp.sum(extra[:, CAP : CAP + 4], axis=0)
    total = sums[0:2] + sums[2:4] * LANES
    top = jnp.floor(total * (1.0 / LANES**2))
    rest = total - top * LANES**2
    middle = jnp.floor(rest * (1.0 / LANES))
    low = rest - middle * LANES
    line = lax.broadcasted_iota(jnp.int32, (blocks * CAP, LANES), 0)
    digits = jnp.zeros((blocks * CAP, LANES), F32)
    for place, value in enumerate((low, middle, top)):
        for lanes in range(2):
            digits = jnp.where(line == 2 * place + lanes, value[lanes : lanes + 1], digits)
    grads_ref[:, 3 * units :] = digits.astype(BF16)
    me = lax.axis_index("dp")
    own_rows_ref[...] = rows_ref[:, pl.ds(pl.multiple_of(me * quarter, LANES), quarter)]
    for step, ref in enumerate(share_refs, 1):
        start = pl.multiple_of(shift(me, step) * quarter, LANES)
        sent = ref.shape[0] - blocks * CAP
        ref[:sent, :quarter] = rows_ref[:sent, pl.ds(start, quarter)]
        ref[sent:, : grads_ref.shape[1]] = grads_ref[...]
    part_dx = dot(grad_in, turned_ref[...], 1, 0)
    part_dx = part_dx.reshape(blocks, CAP, width)
    dx = jnp.concatenate([part_dx[:, :, :half], part_dx[:, :, half:]], axis=1).astype(BF16)
    lane = lax.broadcasted_iota(jnp.int32, (blocks, CAP, LANES), 2)
    tail = jnp.where(lane == 0, part_gate.reshape(blocks, CAP, 1), 0.0)
    tail = jnp.concatenate([tail, jnp.zeros_like(tail)], axis=1).astype(BF16)
    at = 0
    for ref in back_refs:
        ref[:, :, :half] = dx[at : at + ref.shape[0]]
        ref[:, :, half:] = tail[at : at + ref.shape[0]]
        at += ref.shape[0]


def pair_kernel(mine_ref, *refs):
    out_refs = refs[-mine_ref.shape[0] :]
    other = jnp.concatenate([ref[...] for ref in refs[: -len(out_refs)]], axis=0)
    total = mine_ref[...].astype(F32) + other.astype(F32)
    for at, ref in enumerate(out_refs):
        ref[...] = total[at].astype(ref.dtype)


def token_kernel(flights, sel_ref, route_ref, *refs):
    part_refs, (token_ref, gate_ref) = refs[:-2], refs[-2:]
    half = token_ref.shape[1] // 2
    total = 0.0
    for ref in part_refs:
        total = total + jnp.sum(ref[...].astype(F32), axis=1)
    total = total.reshape(flights, BLOCK, half + LANES)
    rows = jnp.concatenate([total[:, :CAP, :half], total[:, CAP:, :half]], axis=2)
    rows = rows.reshape(flights * CAP, 2 * half)
    pick = sel_ref[...]
    if flights == 1:
        token_ref[...] = dot(pick.astype(BF16), rows.astype(BF16), 0, 0).astype(BF16)
    else:
        token_ref[...] = lax.dot_general(
            pick,
            rows,
            (((0,), (0,)), ((), ())),
            precision=lax.Precision.HIGHEST,
            preferred_element_type=F32,
        ).astype(BF16)
    gates = jnp.zeros(gate_ref.shape, F32)
    for flight in range(flights):
        value = jnp.sum(
            pick[flight * CAP : (flight + 1) * CAP] * total[flight, :CAP, half : half + 1],
            axis=0,
            keepdims=True,
        )
        gates = jnp.where(route_ref[...] == flight, value, gates)
    gate_ref[...] = gates


def weight_kernel(units, blocks, copies, bias_ref, *refs):
    given, (gate_ref, up_ref, down_ref, new_ref) = refs[:-4], refs[-4:]
    quarter = gate_ref.shape[1]
    rows, grads = [given[0][...]], [given[1][...]]
    for step, ref in enumerate(given[2 : 1 + copies]):
        sent = ref.shape[0] - blocks * CAP
        rows.append(ref[:sent, :quarter])
        grads.append(ref[sent:, :])
        rows += [other[step, :, :quarter] for other in given[1 + copies :]]
    load = jnp.zeros((2, LANES), F32)
    rows = jnp.concatenate(rows, axis=0)
    hidden, scaled = [], []
    for value in grads:
        value = value.astype(F32)
        digit = value[:CAP, 3 * units :]
        load = load + digit[0:2] + digit[2:4] * LANES + digit[4:6] * LANES**2
        value = value.reshape(blocks, CAP, value.shape[1])
        left, right = value[:, :, : 2 * units], value[:, :, 2 * units : 3 * units]
        left = jnp.concatenate([left, jnp.zeros_like(left)], axis=1)
        right = jnp.concatenate([jnp.zeros_like(right), right], axis=1)
        hidden.append(left.reshape(blocks * BLOCK, 2 * units).astype(BF16))
        scaled.append(right.reshape(blocks * BLOCK, units).astype(BF16))
    both = dot(rows, jnp.concatenate(hidden, axis=0), 0, 0)
    gate_ref[0] = both[:, :units].astype(BF16)
    up_ref[0] = both[:, units:].astype(BF16)
    down_ref[0] = dot(jnp.concatenate(scaled, axis=0), rows, 0, 0).astype(BF16)
    load = jnp.concatenate([load[0:1], load[1:2]], axis=1)
    diff = jnp.sum(load, axis=1, keepdims=True) - EXPERTS_ALL * load
    sign = jnp.where(diff > 0.0, 1.0, jnp.where(diff < 0.0, -1.0, 0.0))
    new_ref[...] = bias_ref[...] + bias_step * sign


def per_device(tokens, out_grad, route, gate_fixed, w_gate, w_up, w_down, router_bias, loads):
    row_count, width = tokens.shape
    top_count = route.shape[1]
    units = w_gate.shape[2]
    sources = lax.axis_size("expert")
    copies = lax.axis_size("dp")
    flights = sources // SPLIT
    half, quarter = width // 2, width // copies
    struct = jax.ShapeDtypeStruct

    given = [tokens, out_grad, route.T, gate_fixed.T, loads]
    payload, pick = call(
        functools.partial(select_kernel, flights),
        [struct((flights, BLOCK, width + LANES), BF16), struct((flights * CAP, row_count), F32)],
        given,
        4 * row_count * width,
        [pltpu.VMEM(a.shape, a.dtype) for a in given] + [pltpu.SemaphoreType.DMA((len(given),))],
        pltpu.HBM,
        60,
    )

    weights = [w_gate[0], w_up[0], w_down[0]]
    weights = call(
        turn_kernel,
        [
            struct((width, 2 * units), BF16),
            struct((width, units), BF16),
            struct((2 * units, width), BF16),
        ],
        weights,
        4 * 10**7,
        limit=16,
        after=[pick],
    )

    def swap(values, step):
        return lax.ppermute(values, "expert", [(i, i ^ step) for i in range(sources)])

    if flights == 1:
        hops = [0, 4, 2, 6]
        near = [payload] + [swap(payload, step) for step in hops[1:]]
        groups = [SPLIT // 2, SPLIT // 2]
    else:
        spread = jnp.broadcast_to(payload[:, None], (flights, SPLIT) + payload.shape[1:])
        spread = spread.reshape((sources,) + payload.shape[1:])
        near = [lax.all_to_all(spread, "expert", split_axis=0, concat_axis=0, tiled=True)]
        groups = [sources]

    paired = copies & (copies - 1) == 0

    def shift(index, step):
        return index ^ step if paired else (index + step) % copies

    def across(values, step):
        return lax.ppermute(values, "dp", [(i, shift(i, step)) for i in range(copies)])

    rows = sources * BLOCK
    kept = groups[0] * BLOCK
    got = near
    if flights == 1:
        got = []
        for part, order, after in ((near[:2], None, ()), (near[2:], [1, 0], weights[2:])):
            got += call(
                functools.partial(stack_kernel, None),
                [struct((len(part),) + payload.shape[1:], BF16)],
                part,
                1000,
                after=after,
                order=order,
            )
        got = got + [swap(value, 1) for value in got]

    wide = max(quarter, 3 * units + LANES)
    outs = call(
        functools.partial(expert_kernel, sources, groups, copies, shift),
        [struct((group, BLOCK, half + LANES), BF16) for group in groups]
        + [struct((kept + sources * CAP, wide), BF16)] * (copies - 1)
        + [struct((rows, quarter), BF16), struct((sources * CAP, 3 * units + LANES), BF16)],
        [*got, *weights],
        4 * 10**7,
        [pltpu.VMEM((rows, width), BF16)],
        limit=18,
    )
    back, shares, own = outs[: len(groups)], outs[len(groups) : -2], outs[-2:]
    shares = [across(value, step) for step, value in enumerate(shares, 1)]

    if flights == 1:
        other = [swap(value, 1) for value in back[1:]]
        block = (BLOCK, half + LANES)
        sums = call(
            pair_kernel,
            [struct(block, F32)] + [struct(block, BF16)] * 3,
            [back[0], *other],
            1000,
        )
        parts = [sums[0]] + [swap(sums[at], hops[at]) for at in range(1, 4)]
        parts = [part.reshape((1, 1) + block) for part in parts]
        (rows_in,) = call(
            functools.partial(stack_kernel, kept),
            [struct((copies - 1, kept, wide), BF16)],
            shares,
            1000,
            after=parts[:0:-1],
            order=[*range(copies - 2, -1, -1)],
        )
        shares = [*shares, swap(rows_in, 1)]
    else:
        parts = lax.all_to_all(back[0], "expert", split_axis=0, concat_axis=0, tiled=True)
        parts = [parts.reshape(flights, SPLIT, BLOCK, half + LANES)]
    grad_gate, grad_up, grad_down, new_bias = call(
        functools.partial(weight_kernel, units, sources, copies),
        [
            struct((1, quarter, units), BF16),
            struct((1, quarter, units), BF16),
            struct((1, units, quarter), BF16),
            struct((1, EXPERTS_ALL), F32),
        ],
        [router_bias[None], *own, *shares],
        1000,
        order=[0, 1, 2, 5, 3, 4, 6] if flights == 1 and copies == 4 else None,
    )
    token_grad, gate_grad = call(
        functools.partial(token_kernel, flights),
        [struct((row_count, width), BF16), struct((top_count, row_count), F32)],
        [pick, route.T] + parts,
        1000,
        order=[0, 1, 2, 5, 3, 4] if flights == 1 else None,
    )
    return (token_grad, gate_grad.T, grad_gate, grad_up, grad_down, new_bias[0])


def solution(mesh):
    in_specs = (
        P(("dp", "expert"), None),
        P(("dp", "expert"), None),
        P(("dp", "expert"), None),
        P(("dp", "expert"), None),
        P("expert", None, None),
        P("expert", None, None),
        P("expert", None, None),
        P(),
        P(("dp", "expert"), None),
    )
    out_specs = (
        P(("dp", "expert"), None),
        P(("dp", "expert"), None),
        P("expert", "dp", None),
        P("expert", "dp", None),
        P("expert", None, "dp"),
        P(),
    )
    return jax.shard_map(
        per_device, mesh=mesh, in_specs=in_specs, out_specs=out_specs, check_vma=False
    )
```

```python
import functools

import jax
import jax.numpy as jnp
from jax import lax
from jax.experimental import pallas as pl
from jax.experimental.pallas import tpu as pltpu
from jax.sharding import PartitionSpec as P

EXPERTS_ALL = 256
SPLIT = 8
CAP = 8
BLOCK = 2 * CAP
LANES = 128
bias_step = 0.125

F32 = jnp.float32
BF16 = jnp.bfloat16


def dot(left, right, left_dim, right_dim):
    return lax.dot_general(
        left, right, (((left_dim,), (right_dim,)), ((), ())), preferred_element_type=F32
    )


def call(kernel, outs, args, cost, scratch=(), space=pltpu.VMEM, limit=6, after=(), order=None):
    if lax.axis_size("expert") > SPLIT:
        limit = 60
    order = order or range(len(args))
    inner = kernel

    def kernel(*refs):
        given = [refs[order.index(at)] for at in range(len(args))]
        inner(*given, *refs[len(args) + len(after) :])

    args = [args[at] for at in order]
    return pl.pallas_call(
        kernel,
        out_shape=outs,
        in_specs=[pl.BlockSpec(memory_space=space)] * len(args)
        + [pl.BlockSpec(memory_space=pl.ANY)] * len(after),
        out_specs=[pl.BlockSpec(memory_space=pltpu.VMEM)] * len(outs),
        scratch_shapes=list(scratch),
        compiler_params=pltpu.CompilerParams(vmem_limit_bytes=limit * 1024 * 1024),
        cost_estimate=pl.CostEstimate(flops=0, bytes_accessed=cost, transcendentals=0),
    )(*args, *after)


def select_kernel(flights, *refs):
    given, (pay_ref, sel_ref), held, sems = refs[:5], refs[5:7], refs[7:12], refs[12]
    copies = [pltpu.make_async_copy(given[at], held[at], sems.at[at]) for at in range(5)]
    for copy in copies:
        copy.start()
    tok_ref, grad_ref, route_ref, fixed_ref, loads_ref = held
    rows, width = tok_ref.shape
    before = lax.broadcasted_iota(jnp.int32, (rows, rows), 0) < lax.broadcasted_iota(
        jnp.int32, (rows, rows), 1
    )
    before = jnp.where(before, 1.0, 0.0).astype(BF16)
    place = lax.broadcasted_iota(jnp.int32, (CAP, rows), 0).astype(F32)
    for copy in copies[2:]:
        copy.wait()
    route, fixed = route_ref[...], fixed_ref[...].astype(F32)
    picks, gates = [], []
    for flight in range(flights):
        hot = route == flight
        mask = jnp.sum(jnp.where(hot, 1.0, 0.0), axis=0, keepdims=True)
        weight = jnp.sum(jnp.where(hot, fixed, 0.0), axis=0, keepdims=True) * (1.0 / 256.0)
        mask = jnp.broadcast_to(mask, (CAP, rows))
        slot = dot(mask.astype(BF16), before, 1, 0)
        pick = jnp.where(slot == place, mask, 0.0)
        picks.append(pick)
        gates.append(jnp.sum(pick * weight, axis=1, keepdims=True))
    pick = jnp.concatenate(picks, axis=0)
    sel_ref[...] = pick
    loads = loads_ref[...]
    high = loads // LANES
    low = (loads - high * LANES).astype(F32)
    high = high.astype(F32)
    line = lax.broadcasted_iota(jnp.int32, (CAP, LANES), 0)
    lane = lax.broadcasted_iota(jnp.int32, (CAP, LANES), 1)
    counts = jnp.zeros((CAP, LANES), F32)
    for at, part in enumerate((low[:, :LANES], low[:, LANES:], high[:, :LANES], high[:, LANES:])):
        counts = jnp.where(line == at, part, counts)
    for flight in range(flights):
        gate = jnp.where(lane == 0, gates[flight], 0.0)
        pay_ref[flight, :, width:] = jnp.concatenate([gate, counts], axis=0).astype(BF16)
    for copy in copies[:2]:
        copy.wait()
    rows_in = dot(pick.astype(BF16), tok_ref[...], 1, 0)
    rows_grad = dot(pick.astype(BF16), grad_ref[...], 1, 0)
    for flight in range(flights):
        own = slice(flight * CAP, (flight + 1) * CAP)
        pay_ref[flight, :, :width] = jnp.concatenate([rows_in[own], rows_grad[own]], axis=0).astype(
            BF16
        )


def stack_kernel(kept, *refs):
    at = 0
    for ref in refs[:-1]:
        value = ref[...] if kept is None else ref[:kept][None]
        refs[-1][at : at + value.shape[0]] = value
        at += value.shape[0]


def turn_kernel(gate_ref, up_ref, down_ref, in_ref, down_turned_ref, in_turned_ref):
    units = gate_ref.shape[1]
    for at, ref in enumerate((gate_ref, up_ref)):
        in_ref[:, at * units : (at + 1) * units] = ref[...]
        in_turned_ref[at * units : (at + 1) * units, :] = ref[...].T
    down_turned_ref[...] = down_ref[...].T


def expert_kernel(blocks, groups, copies, shift, *refs):
    count = 3 + len(groups) + copies + 2
    pay_refs, refs = refs[:-count], refs[-count:]
    (in_ref, down_ref, turned_ref), refs = refs[:3], refs[3:]
    back_refs, share_refs = refs[: len(groups)], refs[len(groups) : -3]
    own_rows_ref, grads_ref, rows_ref = refs[-3:]
    width, units = down_ref.shape
    half = width // 2
    quarter = width // copies
    pays = [ref[...].reshape(-1, ref.shape[-1]) for ref in pay_refs]
    at = 0
    for pay in pays:
        rows_ref[at : at + pay.shape[0], :] = pay[:, :width]
        at += pay.shape[0]
    extra = jnp.concatenate([pay[:, width:] for pay in pays], axis=0).astype(F32)
    extra = extra.reshape(blocks, BLOCK, LANES)
    row_gate = extra[:, :CAP, :1].reshape(blocks * CAP, 1)
    rows = rows_ref[...]

    def part(values, which):
        return values.reshape(blocks, BLOCK, values.shape[-1])[
            :, which * CAP : (which + 1) * CAP
        ].reshape(blocks * CAP, values.shape[-1])

    pre = part(dot(rows, in_ref[...], 1, 0), 0)
    pre_gate, pre_up = pre[:, :units], pre[:, units:]
    back_proj = part(dot(rows, down_ref[...], 1, 0), 1)
    sigmoid_gate = jax.nn.sigmoid(pre_gate)
    activated = pre_gate * sigmoid_gate
    hidden = activated * pre_up
    part_gate = jnp.sum(back_proj * hidden, axis=1, keepdims=True)
    grad_hidden = row_gate * back_proj
    grad_pregate = grad_hidden * pre_up * sigmoid_gate * (1.0 + pre_gate * (1.0 - sigmoid_gate))
    grad_preup = grad_hidden * activated
    scaled_hidden = row_gate * hidden

    grad_in = jnp.concatenate([grad_pregate, grad_preup], axis=1).astype(BF16)
    grads_ref[:, : 2 * units] = grad_in
    grads_ref[:, 2 * units : 3 * units] = scaled_hidden.astype(BF16)
    sums = jnp.sum(extra[:, CAP : CAP + 4], axis=0)
    total = sums[0:2] + sums[2:4] * LANES
    top = jnp.floor(total * (1.0 / LANES**2))
    rest = total - top * LANES**2
    middle = jnp.floor(rest * (1.0 / LANES))
    low = rest - middle * LANES
    line = lax.broadcasted_iota(jnp.int32, (blocks * CAP, LANES), 0)
    digits = jnp.zeros((blocks * CAP, LANES), F32)
    for place, value in enumerate((low, middle, top)):
        for lanes in range(2):
            digits = jnp.where(line == 2 * place + lanes, value[lanes : lanes + 1], digits)
    grads_ref[:, 3 * units :] = digits.astype(BF16)
    me = lax.axis_index("dp")
    own_rows_ref[...] = rows_ref[:, pl.ds(pl.multiple_of(me * quarter, LANES), quarter)]
    for step, ref in enumerate(share_refs, 1):
        start = pl.multiple_of(shift(me, step) * quarter, LANES)
        sent = ref.shape[0] - blocks * CAP
        ref[:sent, :quarter] = rows_ref[:sent, pl.ds(start, quarter)]
        ref[sent:, : grads_ref.shape[1]] = grads_ref[...]
    part_dx = dot(grad_in, turned_ref[...], 1, 0)
    part_dx = part_dx.reshape(blocks, CAP, width)
    dx = jnp.concatenate([part_dx[:, :, :half], part_dx[:, :, half:]], axis=1).astype(BF16)
    lane = lax.broadcasted_iota(jnp.int32, (blocks, CAP, LANES), 2)
    tail = jnp.where(lane == 0, part_gate.reshape(blocks, CAP, 1), 0.0)
    tail = jnp.concatenate([tail, jnp.zeros_like(tail)], axis=1).astype(BF16)
    at = 0
    for ref in back_refs:
        ref[:, :, :half] = dx[at : at + ref.shape[0]]
        ref[:, :, half:] = tail[at : at + ref.shape[0]]
        at += ref.shape[0]


def pair_kernel(mine_ref, *refs):
    out_refs = refs[-mine_ref.shape[0] :]
    other = jnp.concatenate([ref[...] for ref in refs[: -len(out_refs)]], axis=0)
    total = mine_ref[...].astype(F32) + other.astype(F32)
    for at, ref in enumerate(out_refs):
        ref[...] = total[at].astype(ref.dtype)


def token_kernel(flights, sel_ref, route_ref, *refs):
    part_refs, (token_ref, gate_ref) = refs[:-2], refs[-2:]
    half = token_ref.shape[1] // 2
    total = 0.0
    for ref in part_refs:
        total = total + jnp.sum(ref[...].astype(F32), axis=1)
    total = total.reshape(flights, BLOCK, half + LANES)
    rows = jnp.concatenate([total[:, :CAP, :half], total[:, CAP:, :half]], axis=2)
    rows = rows.reshape(flights * CAP, 2 * half)
    pick = sel_ref[...]
    if flights == 1:
        token_ref[...] = dot(pick.astype(BF16), rows.astype(BF16), 0, 0).astype(BF16)
    else:
        token_ref[...] = lax.dot_general(
            pick,
            rows,
            (((0,), (0,)), ((), ())),
            precision=lax.Precision.HIGHEST,
            preferred_element_type=F32,
        ).astype(BF16)
    gates = jnp.zeros(gate_ref.shape, F32)
    for flight in range(flights):
        value = jnp.sum(
            pick[flight * CAP : (flight + 1) * CAP] * total[flight, :CAP, half : half + 1],
            axis=0,
            keepdims=True,
        )
        gates = jnp.where(route_ref[...] == flight, value, gates)
    gate_ref[...] = gates


def weight_kernel(units, blocks, copies, bias_ref, *refs):
    given, (gate_ref, up_ref, down_ref, new_ref) = refs[:-4], refs[-4:]
    quarter = gate_ref.shape[1]
    rows, grads = [given[0][...]], [given[1][...]]
    for step, ref in enumerate(given[2 : 1 + copies]):
        sent = ref.shape[0] - blocks * CAP
        rows.append(ref[:sent, :quarter])
        grads.append(ref[sent:, :])
        rows += [other[step, :, :quarter] for other in given[1 + copies :]]
    load = jnp.zeros((2, LANES), F32)
    rows = jnp.concatenate(rows, axis=0)
    hidden, scaled = [], []
    for value in grads:
        digit = value[:BLOCK].astype(F32)[:CAP, 3 * units :]
        load = load + digit[0:2] + digit[2:4] * LANES + digit[4:6] * LANES**2
        hidden.append(value[:, : 2 * units])
        scaled.append(value[:, 2 * units : 3 * units])
    rows = rows.astype(F32).reshape(-1, BLOCK, quarter)
    rows_in = rows[:, :CAP].reshape(-1, quarter).astype(BF16)
    rows_grad = rows[:, CAP:].reshape(-1, quarter).astype(BF16)
    both = dot(rows_in, jnp.concatenate(hidden, axis=0), 0, 0)
    gate_ref[0] = both[:, :units].astype(BF16)
    up_ref[0] = both[:, units:].astype(BF16)
    down_ref[0] = dot(jnp.concatenate(scaled, axis=0), rows_grad, 0, 0).astype(BF16)
    load = jnp.concatenate([load[0:1], load[1:2]], axis=1)
    diff = jnp.sum(load, axis=1, keepdims=True) - EXPERTS_ALL * load
    sign = jnp.where(diff > 0.0, 1.0, jnp.where(diff < 0.0, -1.0, 0.0))
    new_ref[...] = bias_ref[...] + bias_step * sign


def per_device(tokens, out_grad, route, gate_fixed, w_gate, w_up, w_down, router_bias, loads):
    row_count, width = tokens.shape
    top_count = route.shape[1]
    units = w_gate.shape[2]
    sources = lax.axis_size("expert")
    copies = lax.axis_size("dp")
    flights = sources // SPLIT
    half, quarter = width // 2, width // copies
    struct = jax.ShapeDtypeStruct

    given = [tokens, out_grad, route.T, gate_fixed.T, loads]
    payload, pick = call(
        functools.partial(select_kernel, flights),
        [struct((flights, BLOCK, width + LANES), BF16), struct((flights * CAP, row_count), F32)],
        given,
        4 * row_count * width,
        [pltpu.VMEM(a.shape, a.dtype) for a in given] + [pltpu.SemaphoreType.DMA((len(given),))],
        pltpu.HBM,
        60,
    )

    weights = [w_gate[0], w_up[0], w_down[0]]
    weights = call(
        turn_kernel,
        [
            struct((width, 2 * units), BF16),
            struct((width, units), BF16),
            struct((2 * units, width), BF16),
        ],
        weights,
        4 * 10**7,
        limit=16,
        after=[pick],
    )

    def swap(values, step):
        return lax.ppermute(values, "expert", [(i, i ^ step) for i in range(sources)])

    if flights == 1:
        hops = [0, 4, 2, 6]
        near = [payload] + [swap(payload, step) for step in hops[1:]]
        groups = [SPLIT // 2, SPLIT // 2]
    else:
        spread = jnp.broadcast_to(payload[:, None], (flights, SPLIT) + payload.shape[1:])
        spread = spread.reshape((sources,) + payload.shape[1:])
        near = [lax.all_to_all(spread, "expert", split_axis=0, concat_axis=0, tiled=True)]
        groups = [sources]

    paired = copies & (copies - 1) == 0

    def shift(index, step):
        return index ^ step if paired else (index + step) % copies

    def across(values, step):
        return lax.ppermute(values, "dp", [(i, shift(i, step)) for i in range(copies)])

    rows = sources * BLOCK
    kept = groups[0] * BLOCK
    got = near
    if flights == 1:
        got = []
        for part, order, after in ((near[:2], None, ()), (near[2:], [1, 0], weights[2:])):
            got += call(
                functools.partial(stack_kernel, None),
                [struct((len(part),) + payload.shape[1:], BF16)],
                part,
                1000,
                after=after,
                order=order,
            )
        got = got + [swap(value, 1) for value in got]

    wide = max(quarter, 3 * units + LANES)
    outs = call(
        functools.partial(expert_kernel, sources, groups, copies, shift),
        [struct((group, BLOCK, half + LANES), BF16) for group in groups]
        + [struct((kept + sources * CAP, wide), BF16)] * (copies - 1)
        + [struct((rows, quarter), BF16), struct((sources * CAP, 3 * units + LANES), BF16)],
        [*got, *weights],
        4 * 10**7,
        [pltpu.VMEM((rows, width), BF16)],
        limit=18,
    )
    back, shares, own = outs[: len(groups)], outs[len(groups) : -2], outs[-2:]
    shares = [across(value, step) for step, value in enumerate(shares, 1)]

    if flights == 1:
        other = [swap(value, 1) for value in back[1:]]
        block = (BLOCK, half + LANES)
        sums = call(
            pair_kernel,
            [struct(block, F32)] + [struct(block, BF16)] * 3,
            [back[0], *other],
            1000,
        )
        parts = [sums[0]] + [swap(sums[at], hops[at]) for at in range(1, 4)]
        parts = [part.reshape((1, 1) + block) for part in parts]
        (rows_in,) = call(
            functools.partial(stack_kernel, kept),
            [struct((copies - 1, kept, wide), BF16)],
            shares,
            1000,
            after=parts[:0:-1],
            order=[*range(copies - 2, -1, -1)],
        )
        shares = [*shares, swap(rows_in, 1)]
    else:
        parts = lax.all_to_all(back[0], "expert", split_axis=0, concat_axis=0, tiled=True)
        parts = [parts.reshape(flights, SPLIT, BLOCK, half + LANES)]
    grad_gate, grad_up, grad_down, new_bias = call(
        functools.partial(weight_kernel, units, sources, copies),
        [
            struct((1, quarter, units), BF16),
            struct((1, quarter, units), BF16),
            struct((1, units, quarter), BF16),
            struct((1, EXPERTS_ALL), F32),
        ],
        [router_bias[None], *own, *shares],
        1000,
        order=[0, 1, 2, 5, 3, 4, 6] if flights == 1 and copies == 4 else None,
    )
    token_grad, gate_grad = call(
        functools.partial(token_kernel, flights),
        [struct((row_count, width), BF16), struct((top_count, row_count), F32)],
        [pick, route.T] + parts,
        1000,
        order=[0, 1, 2, 5, 3, 4] if flights == 1 else None,
    )
    return (token_grad, gate_grad.T, grad_gate, grad_up, grad_down, new_bias[0])


def solution(mesh):
    in_specs = (
        P(("dp", "expert"), None),
        P(("dp", "expert"), None),
        P(("dp", "expert"), None),
        P(("dp", "expert"), None),
        P("expert", None, None),
        P("expert", None, None),
        P("expert", None, None),
        P(),
        P(("dp", "expert"), None),
    )
    out_specs = (
        P(("dp", "expert"), None),
        P(("dp", "expert"), None),
        P("expert", "dp", None),
        P("expert", "dp", None),
        P("expert", None, "dp"),
        P(),
    )
    return jax.shard_map(
        per_device, mesh=mesh, in_specs=in_specs, out_specs=out_specs, check_vma=False
    )
```
